128 devices in a mesh: fsdp: 16 (over y, x), tensor: 8 (over z, core).
Axes of the slice: x: 4, y: 4, z: 4, core: 2. Of those that a mesh axis runs over, the one named last changes fastest.
Arguments:
- activations: bfloat16 [4096, 14336], P('fsdp'), may hold values from -6 to 6
- output_grad: bfloat16 [4096, 14336], P('fsdp'), may hold values from -6 to 6
- up_blocks: bfloat16 [8, 192, 128, 128], P('tensor', 'fsdp'), may hold values from -0.5 to 0.5
- up_scale: bfloat16 [8, 192], P('tensor', 'fsdp'), may hold values from 0.25 to 4
- down_blocks: bfloat16 [8, 192, 128, 128], P('tensor', 'fsdp'), may hold values from -0.5 to 0.5
- down_scale: bfloat16 [8, 192], P('tensor', 'fsdp'), may hold values from 0.25 to 4
- up_row_block: int32 [8, 192], P('tensor'), may hold values from 0 to 111, as said below
- up_col_block: int32 [8, 192], P('tensor'), may hold values from 0 to 55
- down_row_block: int32 [8, 192], P('tensor'), may hold values from 0 to 55, as said below
- down_col_block: int32 [8, 192], P('tensor'), may hold values from 0 to 111
- up_count: int32 [8, 16], P('tensor'), may hold values from 2 to 12, as said below
- down_count: int32 [8, 16], P('tensor'), may hold values from 2 to 12, as said below
Outputs:
- input_grad: bfloat16 [4096, 14336], P('fsdp', 'tensor')
- up_grad: bfloat16 [8, 192, 128, 128], P('tensor', 'fsdp')
- down_grad: bfloat16 [8, 192, 128, 128], P('tensor', 'fsdp')
The draws below stay inside these ranges and needn't reach their ends.
Inputs may be any that keep to these rules, and one draw needn't show every extreme that they name: `up_row_block`: within one tensor shard the up slots name distinct block positions, over all 192 slots. `down_row_block`: within one tensor shard the down slots name distinct block positions, over all 192 slots. `up_count`: A slot holds a kept block when its place within its owner is below the owner's count; in every tensor shard some owner holds exactly 12. `down_count`: as for up_count.
All inputs are finite; a program needn't handle non-finite values.
Results may differ from the reference program's by a relative error of at most 0.019.
Values may be sent and summed in bfloat16 or wider, within the bound.
No kernel may reach another device: no remote copies, remote signals or barrier semaphores. Data moves between devices by JAX's collectives and lax.ppermute only.
A program may use at most 256 MiB of HBM per device.

```python
import math
import jax
import jax.numpy as jnp
from jax import lax

D = 14336
FF = 57344
TOK_DEV = 256
CAP = 12
BLK = 128
TOKENS = 4096
FSHARD = 7168
SLOTS = 192
N_FSDP = 16
N_TENSOR = 8


def block_places(key, salt):
    key = jax.random.fold_in(key, salt)
    row_total = D // BLK
    col_total = FF // N_TENSOR // BLK
    place_total = row_total * col_total
    slot_total = N_FSDP * CAP

    def one_shard(subkey):
        first_key, second_key = jax.random.split(subkey)
        scores = jax.random.permutation(first_key, place_total).astype(jnp.int32)
        places = jnp.arange(place_total, dtype=jnp.int32)
        scores = jnp.where(places == 0, -2, jnp.where(places == place_total - 1, -1, scores))
        chosen = jnp.argsort(scores, stable=True)[:slot_total].astype(jnp.int32)
        chosen = jax.random.permutation(second_key, chosen)
        return (chosen // col_total, chosen % col_total)
    shard_keys = jax.random.split(key, N_TENSOR)
    row_pick, col_pick = jax.vmap(one_shard)(shard_keys)
    return (row_pick.astype(jnp.int32), col_pick.astype(jnp.int32))


def skewed_counts(key):
    first_key, second_key = jax.random.split(key)
    lowest = max(1, CAP // 6)
    base = jax.random.randint(first_key, (N_TENSOR, N_FSDP), lowest, CAP // 2 + 1)
    busiest = jax.random.randint(second_key, (N_TENSOR, 1), 0, N_FSDP)
    owners = jnp.arange(N_FSDP, dtype=jnp.int32)[None, :]
    return jnp.where(owners == busiest, CAP, base).astype(jnp.int32)


def draw_up_row_block(key, part):
    row_pick, col_pick = block_places(key, 101)
    return row_pick


def draw_up_col_block(key, part):
    row_pick, col_pick = block_places(key, 101)
    return col_pick


def draw_down_row_block(key, part):
    width_pick, hidden_pick = block_places(key, 202)
    return hidden_pick


def draw_down_col_block(key, part):
    width_pick, hidden_pick = block_places(key, 202)
    return width_pick


def draw_up_count(key, part):
    key = jax.random.fold_in(key, 5)
    return skewed_counts(key)


def draw_down_count(key, part):
    key = jax.random.fold_in(key, 6)
    return skewed_counts(key)


def levels(rng, extent, cuts, least, top_value):
    gain = 1.0
    for dim, parts in cuts:
        steps = jax.random.uniform(jax.random.fold_in(jax.random.fold_in(rng, 6), dim), (parts,), jnp.float32, least / len(cuts), top_value / len(cuts))
        gain = gain * jnp.repeat(jnp.exp(steps), extent[dim] // parts).reshape((-1,) + (1,) * (len(extent) - 1 - dim))
    return gain


def centred(stream_key, dims, deviation, bound, shards=(), kind=jnp.bfloat16):
    drawn = deviation * jax.random.normal(stream_key, dims, jnp.float32)
    if shards:
        drawn = drawn * levels(stream_key, dims, shards, -0.22, 0.18)
    return jnp.clip(drawn, -bound, bound).astype(kind)


def setup_inputs(seed: int = 0) -> dict:
    streams_of = jax.random.split(jax.random.key(seed), 13)
    return {
        "activations": centred(streams_of[0], (TOKENS, D), 1.0, 6.0, ((0, 16),)),
        "output_grad": centred(streams_of[1], (TOKENS, D), 1.0, 6.0, ((0, 16),)),
        "up_blocks": centred(streams_of[2], (N_TENSOR, SLOTS, BLK, BLK), BLK ** -0.5, 0.5, ((0, 8), (1, 16))),
        "up_scale": jnp.clip(jnp.exp(math.log(4.0) - 2.7725887 * jax.random.uniform(streams_of[3], (N_TENSOR, SLOTS), jnp.float32) ** levels(streams_of[3], (N_TENSOR, SLOTS), ((0, 8), (1, 16)), -0.2, 0.2)), 0.25, 4.0).astype(jnp.bfloat16),
        "down_blocks": centred(streams_of[4], (N_TENSOR, SLOTS, BLK, BLK), BLK ** -0.5, 0.5, ((0, 8), (1, 16))),
        "down_scale": jnp.clip(jnp.exp(math.log(4.0) - 2.7725887 * jax.random.uniform(streams_of[5], (N_TENSOR, SLOTS), jnp.float32) ** levels(streams_of[5], (N_TENSOR, SLOTS), ((0, 8), (1, 16)), -0.2, 0.2)), 0.25, 4.0).astype(jnp.bfloat16),
        "up_row_block": draw_up_row_block(jax.random.fold_in(streams_of[12], 71), 0),
        "up_col_block": draw_up_col_block(jax.random.fold_in(streams_of[12], 71), 0),
        "down_row_block": draw_down_row_block(jax.random.fold_in(streams_of[12], 71), 0),
        "down_col_block": draw_down_col_block(jax.random.fold_in(streams_of[12], 71), 0),
        "up_count": draw_up_count(jax.random.fold_in(streams_of[12], 71), 0),
        "down_count": draw_down_count(jax.random.fold_in(streams_of[12], 71), 0),
    }


ROOT_TWO_PI = 0.7978845608028654
CUBIC = 0.044715


def gelu_parts(hidden):
    tangent = jnp.tanh(ROOT_TWO_PI * (hidden + CUBIC * hidden * hidden * hidden))
    gelu_value = 0.5 * hidden * (1.0 + tangent)
    gelu_slope = 0.5 * (1.0 + tangent) + 0.5 * hidden * (1.0 - tangent * tangent) * ROOT_TWO_PI * (1.0 + 3.0 * CUBIC * hidden * hidden)
    return gelu_value, gelu_slope


def rounded(values):
    return lax.optimization_barrier(values.astype(jnp.bfloat16)).astype(jnp.float32)


def reference(activations, output_grad, up_blocks, up_scale, down_blocks, down_scale, up_row_block, up_col_block, down_row_block, down_col_block, up_count, down_count):
    row_blocks = D // BLK
    col_blocks = FSHARD // BLK
    slot_total = N_FSDP * CAP
    acts_three = activations.reshape(TOKENS, row_blocks, BLK)
    grads_three = output_grad.reshape(TOKENS, row_blocks, BLK)
    slot_index = jnp.arange(slot_total)
    grad_norm = float(TOKENS) ** -0.5
    input_total = jnp.zeros((TOKENS, row_blocks, BLK), jnp.float32)
    up_list = []
    down_list = []
    for shard in range(N_TENSOR):
        up_live = (slot_index % CAP < jnp.repeat(up_count[shard], CAP)).astype(jnp.float32)
        down_live = (slot_index % CAP < jnp.repeat(down_count[shard], CAP)).astype(jnp.float32)
        up_factor = up_scale[shard].astype(jnp.float32) * up_live
        down_factor = down_scale[shard].astype(jnp.float32) * down_live

        def forward_step(carry, item):
            hidden, backed = carry
            up_tile, up_mult, up_row, up_col, down_tile, down_mult, down_row, down_col = item
            source = lax.dynamic_index_in_dim(acts_three, up_row, 1, keepdims=False)
            hidden = hidden.at[up_col].add(up_mult * jnp.dot(source, up_tile, preferred_element_type=jnp.float32))
            target = lax.dynamic_index_in_dim(grads_three, down_col, 1, keepdims=False)
            backed = backed.at[down_row].add(down_mult * jnp.dot(target, down_tile.T, preferred_element_type=jnp.float32))
            return (hidden, backed), None

        empty = jnp.zeros((col_blocks, TOKENS, BLK), jnp.float32)
        items = (up_blocks[shard], up_factor, up_row_block[shard], up_col_block[shard], down_blocks[shard], down_factor, down_row_block[shard], down_col_block[shard])
        (hidden, backed), unused = lax.scan(forward_step, (empty, empty), items)
        gelu_value, gelu_slope = gelu_parts(hidden)
        activated = gelu_value.astype(jnp.bfloat16)
        hidden_grad = (backed * gelu_slope).astype(jnp.bfloat16)

        def input_step(partial_sum, item):
            up_tile, up_mult, up_row, up_col = item
            source = lax.dynamic_index_in_dim(hidden_grad, up_col, 0, keepdims=False)
            product = up_mult * jnp.dot(source, up_tile.T, preferred_element_type=jnp.float32)
            return partial_sum.at[:, up_row].add(product), None

        partial_sum, unused = lax.scan(input_step, jnp.zeros((TOKENS, row_blocks, BLK), jnp.float32), items[:4])
        input_total = input_total + rounded(partial_sum)

        def block_grads(item):
            up_row, up_col, down_row, down_col = item
            left = lax.dynamic_index_in_dim(acts_three, up_row, 1, keepdims=False).astype(jnp.float32).reshape(N_FSDP, TOK_DEV, BLK)
            right = lax.dynamic_index_in_dim(hidden_grad, up_col, 0, keepdims=False).astype(jnp.float32).reshape(N_FSDP, TOK_DEV, BLK)
            up_term = jnp.einsum("gti,gtj->gij", left, right, precision=lax.Precision.HIGHEST)
            left = lax.dynamic_index_in_dim(activated, down_row, 0, keepdims=False).astype(jnp.float32).reshape(N_FSDP, TOK_DEV, BLK)
            right = lax.dynamic_index_in_dim(grads_three, down_col, 1, keepdims=False).astype(jnp.float32).reshape(N_FSDP, TOK_DEV, BLK)
            down_term = jnp.einsum("gti,gtj->gij", left, right, precision=lax.Precision.HIGHEST)
            return jnp.sum(rounded(up_term), axis=0), jnp.sum(rounded(down_term), axis=0)

        up_sum, down_sum = lax.map(block_grads, (up_row_block[shard], up_col_block[shard], down_row_block[shard], down_col_block[shard]))
        up_list.append((up_sum * (up_factor * grad_norm)[:, None, None]).astype(jnp.bfloat16))
        down_list.append((down_sum * (down_factor * grad_norm)[:, None, None]).astype(jnp.bfloat16))
    input_grad = input_total.astype(jnp.bfloat16).reshape(TOKENS, D)
    return input_grad, jnp.stack(up_list), jnp.stack(down_list)
```

```python
import jax
import jax.numpy as jnp
from jax import lax
from jax.experimental import pallas as pl
from jax.experimental.pallas import tpu as pltpu
from jax.sharding import PartitionSpec as P

FF = 57344


ROOT_TWO_PI = 0.7978845608028654
CUBIC = 0.044715


def gelu_parts(hidden):
    tangent = jnp.tanh(ROOT_TWO_PI * (hidden + CUBIC * hidden * hidden * hidden))
    gelu_value = 0.5 * hidden * (1.0 + tangent)
    gelu_slope = 0.5 * (1.0 + tangent) + 0.5 * hidden * (1.0 - tangent * tangent) * ROOT_TWO_PI * (
        1.0 + 3.0 * CUBIC * hidden * hidden
    )
    return (gelu_value, gelu_slope)


def pick_matrix(indices, count, kind):
    return (indices[:, None] == jnp.arange(count, dtype=jnp.int32)[None, :]).astype(kind)


def pick_middle(table, indices):
    selector = pick_matrix(indices, table.shape[1], jnp.bfloat16)
    return jnp.einsum("trb,mr->tmb", table, selector, preferred_element_type=jnp.float32).astype(
        jnp.bfloat16
    )


def pick_front(table, indices):
    selector = pick_matrix(indices, table.shape[0], jnp.bfloat16)
    return jnp.einsum("ctb,mc->mtb", table, selector, preferred_element_type=jnp.float32).astype(
        jnp.bfloat16
    )


def full_exchange(
    activations,
    output_grad,
    up_blocks,
    up_scale,
    down_blocks,
    down_scale,
    up_row_block,
    up_col_block,
    down_row_block,
    down_col_block,
    up_count,
    down_count,
):
    token_rows = activations.shape[0]
    block_size = up_blocks.shape[2]
    capacity = up_blocks.shape[1]
    owners = lax.axis_size("fsdp")
    slot_total = owners * capacity
    row_blocks = activations.shape[1] // block_size
    col_blocks = FF // lax.axis_size("tensor") // block_size
    acts_three = activations.reshape(token_rows, row_blocks, block_size)
    grads_three = output_grad.reshape(token_rows, row_blocks, block_size)
    slot_index = jnp.arange(slot_total)
    up_live = (slot_index % capacity < jnp.repeat(up_count[0], capacity)).astype(jnp.float32)
    down_live = (slot_index % capacity < jnp.repeat(down_count[0], capacity)).astype(jnp.float32)
    up_rows = up_row_block[0]
    up_cols = up_col_block[0]
    down_rows = down_row_block[0]
    down_cols = down_col_block[0]
    grad_norm = float(token_rows * owners) ** (-0.5)
    up_tiles = lax.all_gather(up_blocks, "fsdp", axis=1, tiled=True)
    up_mults = lax.all_gather(up_scale, "fsdp", axis=1, tiled=True)
    down_tiles = lax.all_gather(down_blocks, "fsdp", axis=1, tiled=True)
    down_mults = lax.all_gather(down_scale, "fsdp", axis=1, tiled=True)
    row_pick = up_rows
    col_pick = up_cols
    factor = up_mults[0].astype(jnp.float32) * up_live
    source = pick_middle(acts_three, row_pick)
    product = jnp.einsum("tmi,mij->mtj", source, up_tiles[0], preferred_element_type=jnp.float32)
    placing = pick_matrix(col_pick, col_blocks, jnp.float32) * factor[:, None]
    hidden = jnp.einsum("mc,mtj->ctj", placing, product, precision=lax.Precision.HIGHEST)
    row_pick = down_rows
    col_pick = down_cols
    factor = down_mults[0].astype(jnp.float32) * down_live
    target = pick_middle(grads_three, col_pick)
    product = jnp.einsum("tmj,mij->mti", target, down_tiles[0], preferred_element_type=jnp.float32)
    placing = pick_matrix(row_pick, col_blocks, jnp.float32) * factor[:, None]
    backed = jnp.einsum("mc,mti->cti", placing, product, precision=lax.Precision.HIGHEST)
    hidden, backed = (hidden, backed)
    gelu_value, gelu_slope = gelu_parts(hidden)
    activated = gelu_value.astype(jnp.bfloat16)
    hidden_grad = (backed * gelu_slope).astype(jnp.bfloat16)
    up_tiles = lax.all_gather(up_blocks, "fsdp", axis=1, tiled=True)
    up_mults = lax.all_gather(up_scale, "fsdp", axis=1, tiled=True)
    row_pick = up_rows
    col_pick = up_cols
    factor = up_mults[0].astype(jnp.float32) * up_live
    source = pick_front(hidden_grad, col_pick)
    product = jnp.einsum("mtj,mij->tmi", source, up_tiles[0], preferred_element_type=jnp.float32)
    placing = pick_matrix(row_pick, row_blocks, jnp.float32) * factor[:, None]
    partial_sum = jnp.einsum("tmi,mr->tri", product, placing, precision=lax.Precision.HIGHEST)
    row_pick = up_rows
    col_pick = up_cols
    left_side = pick_middle(acts_three, row_pick)
    right_side = pick_front(hidden_grad, col_pick)
    row_pick = down_rows
    col_pick = down_cols
    down_left_side = pick_front(activated, row_pick)
    down_right_side = pick_middle(grads_three, col_pick)
    summed = lax.psum_scatter(
        jnp.stack(
            [
                jnp.einsum(
                    "tmi,mtj->mij", left_side, right_side, preferred_element_type=jnp.float32
                ),
                jnp.einsum(
                    "mti,tmj->mij",
                    down_left_side,
                    down_right_side,
                    preferred_element_type=jnp.float32,
                ),
            ],
            axis=1,
        ).astype(jnp.bfloat16),
        "fsdp",
        scatter_dimension=0,
        tiled=True,
    ).astype(jnp.float32)
    up_summed = summed[:, 0]
    down_summed = summed[:, 1]
    own_start = lax.axis_index("fsdp") * capacity
    up_factor = up_scale[0].astype(jnp.float32) * lax.dynamic_slice_in_dim(
        up_live, own_start, capacity
    )
    down_factor = down_scale[0].astype(jnp.float32) * lax.dynamic_slice_in_dim(
        down_live, own_start, capacity
    )
    up_grad = (up_summed * (up_factor * grad_norm)[:, None, None]).astype(jnp.bfloat16)[None]
    down_grad = (down_summed * (down_factor * grad_norm)[:, None, None]).astype(jnp.bfloat16)[None]
    flat_sum = partial_sum.reshape(token_rows, row_blocks * block_size)
    input_grad = lax.psum_scatter(
        flat_sum.astype(jnp.bfloat16), "tensor", scatter_dimension=1, tiled=True
    )
    return (input_grad, up_grad, down_grad)


SIDE = 4
CAP = 12
BLK = 128
ROOM = 30
LIST = 128
VMEM_LIMIT = 60 * 1024 * 1024


def shift_x(step):
    return [(y * SIDE + x, y * SIDE + (x + step) % SIDE) for y in range(SIDE) for x in range(SIDE)]


def shift_y(step):
    return [(y * SIDE + x, (y + step) % SIDE * SIDE + x) for y in range(SIDE) for x in range(SIDE)]


def back(place, step):
    return lax.rem(place + SIDE - step, SIDE)


def any_tensor(flag):
    def moved(pairs):
        return lax.ppermute(flag, "tensor", pairs)

    flag = jnp.maximum(flag, moved([(t, t ^ 1) for t in range(8)]))
    flag = jnp.maximum(flag, moved([(t, (t + 2) % 8) for t in range(8)]))
    return jnp.maximum(flag, moved([(t, (t + 4) % 8) for t in range(8)]))


def up_owner(y, x, far, near):
    return back(y, far) * SIDE + back(x, near)


def down_owner(y, x, far, near):
    return back(y, near) * SIDE + back(x, far)


def call(kernel, outs, in_spaces, out_spaces, scratch, name, cost=None):
    return pl.pallas_call(
        kernel,
        out_shape=outs,
        in_specs=[pl.BlockSpec(memory_space=s) for s in in_spaces],
        out_specs=[pl.BlockSpec(memory_space=s) for s in out_spaces],
        scratch_shapes=scratch,
        compiler_params=pltpu.CompilerParams(vmem_limit_bytes=VMEM_LIMIT),
        cost_estimate=cost,
        name=name,
    )


V, S, A = pltpu.VMEM, pltpu.SMEM, pl.ANY


def cost(us):
    return pl.CostEstimate(flops=0, bytes_accessed=int(us * 3e6), transcendentals=0)


def blocks(count):
    return jax.ShapeDtypeStruct((count, BLK, BLK), jnp.bfloat16)


def pack_kernel(place, up_count, down_count, *refs):
    y, x = place[0], place[1]
    for owner_of, count, ins, out in (
        (up_owner, up_count, refs[:4], refs[8]),
        (down_owner, down_count, refs[4:8], refs[9]),
    ):
        position = 0
        for near in range(SIDE):
            live = count[owner_of(y, x, 0, near)]

            def put(j, at, source=ins[near], out=out):
                out[at] = source[j]
                return at + 1

            position = lax.fori_loop(0, live, put, position)


def table_kernel(place, up_count, up_row, up_col, down_count, down_row, down_col, table):
    y, x = place[0], place[1]
    for first, owner_of, count, rows, cols in (
        (0, up_owner, up_count, up_row, up_col),
        (3, down_owner, down_count, down_row, down_col),
    ):
        def blank(i, unused, first=first):
            table[first, i] = SIDE * ROOM
            table[first + 1, i] = 0
            table[first + 2, i] = 0
            return unused

        total = 0
        for far in range(SIDE):
            position = far * ROOM
            for near in range(SIDE):
                owner = owner_of(y, x, far, near)
                live = count[owner]

                def note(j, unused, first=first, rows=rows, cols=cols, owner=owner, total=total, position=position):
                    table[first, total + j] = position + j
                    table[first + 1, total + j] = rows[owner * CAP + j]
                    table[first + 2, total + j] = cols[owner * CAP + j]
                    return unused

                lax.fori_loop(0, live, note, 0)
                total = total + live
                position = position + live
        padded = (total + 3) // 4
        lax.fori_loop(total, padded * 4, blank, 0)
        table[6, first] = padded


def lane(index):
    return pl.ds(pl.multiple_of(index * BLK, BLK), BLK)


def forward_kernel(table, acts, grads, *refs):
    ups, downs = refs[:4], refs[4:8]
    activated, hidden_grad = refs[8:10]
    up_tiles, down_tiles, hidden, backed, sems = refs[10:]
    copies = []
    for far in range(SIDE):
        for which, (source, target) in enumerate(((ups[far], up_tiles), (downs[far], down_tiles))):
            copy = pltpu.make_async_copy(
                source, target.at[pl.ds(far * ROOM, ROOM)], sems.at[which, far]
            )
            copy.start()
            copies.append(copy)
    up_tiles[SIDE * ROOM] = jnp.zeros((BLK, BLK), jnp.bfloat16)
    down_tiles[SIDE * ROOM] = jnp.zeros((BLK, BLK), jnp.bfloat16)
    hidden[...] = jnp.zeros_like(hidden)
    backed[...] = jnp.zeros_like(backed)
    for copy in copies:
        copy.wait()

    def up_step(i, unused):
        products = []
        for u in range(4):
            at = i * 4 + u
            products.append(
                jnp.dot(acts[:, lane(table[1, at])], up_tiles[table[0, at]], preferred_element_type=jnp.float32)
            )
        for u in range(4):
            hidden[:, lane(table[2, i * 4 + u])] += products[u]
        return unused

    lax.fori_loop(0, table[6, 0], up_step, 0)

    def down_step(i, unused):
        products = []
        for u in range(4):
            at = i * 4 + u
            products.append(
                lax.dot_general(
                    grads[:, lane(table[5, at])],
                    down_tiles[table[3, at]],
                    (((1,), (1,)), ((), ())),
                    preferred_element_type=jnp.float32,
                )
            )
        for u in range(4):
            backed[:, lane(table[4, i * 4 + u])] += products[u]
        return unused

    lax.fori_loop(0, table[6, 3], down_step, 0)

    def bend(i, unused):
        value, slope = gelu_parts(hidden[:, lane(i)])
        activated[:, lane(i)] = value.astype(jnp.bfloat16)
        hidden_grad[:, lane(i)] = (backed[:, lane(i)] * slope).astype(jnp.bfloat16)
        return unused

    lax.fori_loop(0, hidden.shape[1] // BLK, bend, 0)


def terms_kernel(table, acts, grads, activated, hidden_grad, *refs):
    outs = refs[:8]
    up_terms, down_terms, sems = refs[8:]

    def step(first, left, right, terms):
        def body(i, unused):
            for u in range(4):
                at = i * 4 + u
                terms[table[first, at]] = lax.dot_general(
                    left[:, lane(table[first + 1, at])],
                    right[:, lane(table[first + 2, at])],
                    (((0,), (0,)), ((), ())),
                    preferred_element_type=jnp.float32,
                ).astype(jnp.bfloat16)
            return unused

        lax.fori_loop(0, table[6, first], body, 0)

    copies = []

    def send(which, terms):
        for far in range(SIDE):
            copy = pltpu.make_async_copy(
                terms.at[pl.ds(far * ROOM, ROOM)], outs[which * 4 + far], sems.at[which, far]
            )
            copy.start()
            copies.append(copy)

    step(0, acts, hidden_grad, up_terms)
    send(0, up_terms)
    step(3, activated, grads, down_terms)
    send(1, down_terms)
    for copy in copies:
        copy.wait()


def partial_kernel(table, hidden_grad, *refs):
    ups, out = refs[:4], refs[4]
    up_tiles, partial, sems = refs[5:]
    copies = []
    for far in range(SIDE):
        copy = pltpu.make_async_copy(ups[far], up_tiles.at[pl.ds(far * ROOM, ROOM)], sems.at[far])
        copy.start()
        copies.append(copy)
    up_tiles[SIDE * ROOM] = jnp.zeros((BLK, BLK), jnp.bfloat16)
    partial[...] = jnp.zeros_like(partial)
    for copy in copies:
        copy.wait()

    def step(i, unused):
        products = []
        for u in range(4):
            at = i * 4 + u
            products.append(
                lax.dot_general(
                    hidden_grad[:, lane(table[2, at])],
                    up_tiles[table[0, at]],
                    (((1,), (1,)), ((), ())),
                    preferred_element_type=jnp.float32,
                )
            )
        for u in range(4):
            partial[:, lane(table[1, i * 4 + u])] += products[u]
        return unused

    lax.fori_loop(0, table[6, 0], step, 0)

    def write(i, unused):
        out[:, lane(i)] = partial[:, lane(i)].astype(jnp.bfloat16)
        return unused

    lax.fori_loop(0, partial.shape[1] // BLK, write, 0)


def unpack_kernel(place, up_count, down_count, *refs):
    y, x = place[0], place[1]
    for owner_of, count, ins, outs in (
        (up_owner, up_count, refs[:4], refs[8:12]),
        (down_owner, down_count, refs[4:8], refs[12:16]),
    ):
        position = 0
        for near in range(SIDE):
            live = count[owner_of(y, x, 0, near)]

            def put(j, at, ins=ins, out=outs[near]):
                out[j] = sum(ref[at].astype(jnp.float32) for ref in ins).astype(jnp.bfloat16)
                return at + 1

            position = lax.fori_loop(0, live, put, position)


def finish_kernel(place, up_count, down_count, up_factor, down_factor, *refs):
    owner = place[0] * SIDE + place[1]
    for count, factor, ins, out in (
        (up_count, up_factor, refs[:4], refs[8]),
        (down_count, down_factor, refs[4:8], refs[9]),
    ):
        live = count[owner]

        def put(j, unused, ins=ins, out=out, factor=factor):
            out[j] = (sum(ref[j].astype(jnp.float32) for ref in ins) * factor[j]).astype(jnp.bfloat16)
            return unused

        def clear(j, unused, out=out):
            out[j] = jnp.zeros((BLK, BLK), jnp.bfloat16)
            return unused

        lax.fori_loop(0, live, put, 0)
        lax.fori_loop(live, CAP, clear, 0)


def packed_exchange(near_up, near_down, activations, output_grad, up_blocks, up_scale, down_blocks, down_scale,
                    up_row_block, up_col_block, down_row_block, down_col_block, up_count, down_count):
    tokens = activations.shape[0]
    width = activations.shape[1]
    hidden_width = FF // lax.axis_size("tensor")
    grad_norm = float(tokens * lax.axis_size("fsdp")) ** (-0.5)
    me = lax.axis_index("fsdp")
    place = jnp.stack([me // SIDE, me % SIDE]).astype(jnp.int32)
    up_count, down_count = up_count[0], down_count[0]
    packed_up, packed_down = call(
        pack_kernel, [blocks(ROOM)] * 2, [S] * 3 + [V] * 8, [V] * 2, [], "pack", cost(2)
    )(place, up_count, down_count, *near_up, *near_down)
    far_up = [packed_up] + [lax.ppermute(packed_up, "fsdp", shift_y(m)) for m in range(1, SIDE)]
    far_down = [packed_down] + [lax.ppermute(packed_down, "fsdp", shift_x(m)) for m in range(1, SIDE)]
    (table,) = call(
        table_kernel, [jax.ShapeDtypeStruct((8, LIST), jnp.int32)], [S] * 7, [S], [], "table", cost(2)
    )(place, up_count, up_row_block[0], up_col_block[0], down_count, down_row_block[0], down_col_block[0])
    half = jax.ShapeDtypeStruct((tokens, hidden_width), jnp.bfloat16)
    tiles = pltpu.VMEM((SIDE * ROOM + 1, BLK, BLK), jnp.bfloat16)
    activated, hidden_grad = call(
        forward_kernel,
        [half, half],
        [S, V, V] + [A] * 8,
        [V, V],
        [tiles, tiles]
        + [pltpu.VMEM((tokens, hidden_width), jnp.float32)] * 2
        + [pltpu.SemaphoreType.DMA((2, SIDE))],
        "forward", cost(25),
    )(table, activations, output_grad, *far_up, *far_down)
    terms = call(
        terms_kernel,
        [blocks(ROOM)] * 8,
        [S, V, V, V, V],
        [A] * 8,
        [tiles, tiles, pltpu.SemaphoreType.DMA((2, SIDE))],
        "terms", cost(20),
    )(table, activations, output_grad, activated, hidden_grad)
    up_terms = [terms[0]] + [lax.ppermute(terms[m], "fsdp", shift_y(SIDE - m)) for m in range(1, SIDE)]
    down_terms = [terms[4]] + [lax.ppermute(terms[4 + m], "fsdp", shift_x(SIDE - m)) for m in range(1, SIDE)]
    (partial,) = call(
        partial_kernel,
        [jax.ShapeDtypeStruct((tokens, width), jnp.bfloat16)],
        [S, V] + [A] * 4,
        [V],
        [tiles, pltpu.VMEM((tokens, width), jnp.float32), pltpu.SemaphoreType.DMA((SIDE,))],
        "partial", cost(15),
    )(table, hidden_grad, *far_up)
    input_grad = lax.psum_scatter(partial, "tensor", scatter_dimension=1, tiled=True)
    sums = call(
        unpack_kernel, [blocks(CAP)] * 8, [S] * 3 + [V] * 8, [V] * 8, [], "unpack", cost(3)
    )(place, up_count, down_count, *up_terms, *down_terms)
    near_up = [sums[0]] + [lax.ppermute(sums[k], "fsdp", shift_x(SIDE - k)) for k in range(1, SIDE)]
    near_down = [sums[4]] + [lax.ppermute(sums[4 + k], "fsdp", shift_y(SIDE - k)) for k in range(1, SIDE)]
    up_grad, down_grad = call(
        finish_kernel, [blocks(CAP)] * 2, [S] * 5 + [V] * 8, [V] * 2, [], "finish", cost(3)
    )(
        place, up_count, down_count,
        up_scale[0].astype(jnp.float32) * grad_norm,
        down_scale[0].astype(jnp.float32) * grad_norm,
        *near_up, *near_down,
    )
    return input_grad, up_grad[None], down_grad[None]


def on_device(*args):
    up_blocks, up_scale, down_blocks, down_scale = args[2:6]
    up_live = args[10][0].reshape(SIDE, SIDE).sum(1).max()
    down_live = args[11][0].reshape(SIDE, SIDE).sum(0).max()
    crowded = any_tensor(jnp.maximum(up_live, down_live).reshape(1))[0] > ROOM
    scaled_up = up_blocks[0] * up_scale[0][:, None, None]
    scaled_down = down_blocks[0] * down_scale[0][:, None, None]
    near_up = [scaled_up] + [lax.ppermute(scaled_up, "fsdp", shift_x(k)) for k in range(1, SIDE)]
    near_down = [scaled_down] + [lax.ppermute(scaled_down, "fsdp", shift_y(k)) for k in range(1, SIDE)]
    return lax.cond(
        crowded,
        lambda near_up, near_down, *rest: full_exchange(*rest),
        packed_exchange,
        near_up, near_down, *args,
    )


def solution(mesh):
    return jax.shard_map(
        on_device,
        mesh=mesh,
        in_specs=(
            P("fsdp", None),
            P("fsdp", None),
            P("tensor", "fsdp", None, None),
            P("tensor", "fsdp"),
            P("tensor", "fsdp", None, None),
            P("tensor", "fsdp"),
            P("tensor", None),
            P("tensor", None),
            P("tensor", None),
            P("tensor", None),
            P("tensor", None),
            P("tensor", None),
        ),
        out_specs=(
            P("fsdp", "tensor"),
            P("tensor", "fsdp", None, None),
            P("tensor", "fsdp", None, None),
        ),
        check_vma=False,
    )
```

```python
import jax
import jax.numpy as jnp
from jax import lax
from jax.experimental import pallas as pl
from jax.experimental.pallas import tpu as pltpu
from jax.sharding import PartitionSpec as P

FF = 57344


ROOT_TWO_PI = 0.7978845608028654
CUBIC = 0.044715


def gelu_parts(hidden):
    tangent = jnp.tanh(ROOT_TWO_PI * (hidden + CUBIC * hidden * hidden * hidden))
    gelu_value = 0.5 * hidden * (1.0 + tangent)
    gelu_slope = 0.5 * (1.0 + tangent) + 0.5 * hidden * (1.0 - tangent * tangent) * ROOT_TWO_PI * (
        1.0 + 3.0 * CUBIC * hidden * hidden
    )
    return (gelu_value, gelu_slope)


SIDE = 4
CAP = 12
BLK = 128
ROOM = 30
LIST = 192
VMEM_LIMIT = 60 * 1024 * 1024
V, S, A = pltpu.VMEM, pltpu.SMEM, pl.ANY


def shift_x(step):
    return [(y * SIDE + x, y * SIDE + (x + step) % SIDE) for y in range(SIDE) for x in range(SIDE)]


def shift_y(step):
    return [(y * SIDE + x, (y + step) % SIDE * SIDE + x) for y in range(SIDE) for x in range(SIDE)]


def shift_z(step):
    return [(z * 2 + c, (z + step) % SIDE * 2 + c) for z in range(SIDE) for c in range(2)]


def along(axis, shift):
    return lambda array, step: lax.ppermute(array, axis, shift(step))


over_x, over_y, over_z = along("fsdp", shift_x), along("fsdp", shift_y), along("tensor", shift_z)


def back(place, step):
    return lax.rem(place + SIDE - step, SIDE)


def any_tensor(flag):
    def moved(pairs):
        return lax.ppermute(flag, "tensor", pairs)

    flag = jnp.maximum(flag, moved([(t, t ^ 1) for t in range(8)]))
    flag = jnp.maximum(flag, moved([(t, (t + 2) % 8) for t in range(8)]))
    return jnp.maximum(flag, moved([(t, (t + 4) % 8) for t in range(8)]))


def spread(rings, flag=None):
    half = rings[0][0].shape[0] // 2
    first = [(move(own, 1), move(own, 3)) for own, move in rings]
    if flag is not None:
        first, flag = lax.optimization_barrier((first, any_tensor(flag)))
    second = [
        (move(one[:half], 1), move(three[half:], 3))
        for (own, move), (one, three) in zip(rings, first)
    ]
    spreads = [
        (own, one, low, high, three)
        for (own, move), (one, three), (low, high) in zip(rings, first, second)
    ]
    return spreads if flag is None else (spreads, flag)


def add(*arrays):
    return sum(a.astype(jnp.float32) for a in arrays).astype(jnp.bfloat16)


def collect(rings):
    half = rings[0][3].shape[0]
    first = [(move(back, 3), move(fore, 1)) for own, back, fore, one, three, move in rings]
    second = [
        (move(add(one, from_fore[:half]), 3), move(add(three, from_back[:half]), 1))
        for (own, back, fore, one, three, move), (from_fore, from_back) in zip(rings, first)
    ]
    return [(ring[0],) + f + s for ring, f, s in zip(rings, first, second)]


def up_owner(y, x, far, near):
    return back(y, far) * SIDE + back(x, near)


def down_owner(y, x, far, near):
    return back(y, near) * SIDE + back(x, far)


def cost(us):
    return pl.CostEstimate(flops=0, bytes_accessed=int(us * 3e6), transcendentals=0)


def call(kernel, outs, in_spaces, out_spaces, scratch, name, us):
    return pl.pallas_call(
        kernel,
        out_shape=outs,
        in_specs=[pl.BlockSpec(memory_space=s) for s in in_spaces],
        out_specs=[pl.BlockSpec(memory_space=s) for s in out_spaces],
        scratch_shapes=scratch,
        compiler_params=pltpu.CompilerParams(vmem_limit_bytes=VMEM_LIMIT),
        cost_estimate=cost(us),
        name=name,
    )


def blocks(count):
    return jax.ShapeDtypeStruct((count, BLK, BLK), jnp.bfloat16)


def pieces(size):
    half = size // 2
    return ((0, 0, size), (1, 0, size), (2, 0, half), (2, half, half), (3, 0, size))


def pack_kernel(room, place, up_count, down_count, *refs):
    y, x = place[0], place[1]
    for owner_of, count, ins, out in (
        (up_owner, up_count, refs[:5], refs[10]),
        (down_owner, down_count, refs[5:10], refs[11]),
    ):
        position = 0
        for (near, first, size), source in zip(pieces(CAP), ins):
            live = jnp.clip(count[owner_of(y, x, 0, near)] - first, 0, size)
            live = jnp.minimum(live, room - position)

            def put(j, at, source=source, out=out):
                out[at] = source[j]
                return at + 1

            position = lax.fori_loop(0, live, put, position)


def table_kernel(room, place, up_count, up_row, up_col, down_count, down_row, down_col, table, most):
    y, x = place[0], place[1]
    largest = 0
    for first, owner_of, count, rows, cols in (
        (0, up_owner, up_count, up_row, up_col),
        (3, down_owner, down_count, down_row, down_col),
    ):
        def blank(i, unused, first=first):
            table[first, i] = SIDE * room
            table[first + 1, i] = 0
            table[first + 2, i] = 0
            return unused

        total = 0
        for far in range(SIDE):
            position = far * room
            wanted = 0
            for near in range(SIDE):
                owner = owner_of(y, x, far, near)
                wanted = wanted + count[owner]
                live = jnp.minimum(count[owner], (far + 1) * room - position)

                def note(j, unused, first=first, rows=rows, cols=cols, owner=owner, total=total, position=position):
                    table[first, total + j] = position + j
                    table[first + 1, total + j] = rows[owner * CAP + j]
                    table[first + 2, total + j] = cols[owner * CAP + j]
                    return unused

                lax.fori_loop(0, live, note, 0)
                total = total + live
                position = position + live
            largest = jnp.maximum(largest, wanted)
        padded = (total + 3) // 4
        lax.fori_loop(total, padded * 4, blank, 0)
        table[6, first] = padded
    most[0] = largest


def make_table(room, place, up_count, up_row, up_col, down_count, down_row, down_col):
    def kernel(*refs):
        table_kernel(room, *refs)

    outs = [jax.ShapeDtypeStruct((8, LIST), jnp.int32), jax.ShapeDtypeStruct((1,), jnp.int32)]
    return call(kernel, outs, [S] * 7, [S] * 2, [], "table", 3)(
        place, up_count, up_row, up_col, down_count, down_row, down_col
    )


def lane(index):
    return pl.ds(pl.multiple_of(index * BLK, BLK), BLK)


def block_products(table, first, take, give, left, tiles, out, contract, offset=0):
    def step(i, unused):
        products = []
        for u in range(4):
            at = i * 4 + u
            products.append(
                lax.dot_general(
                    left[:, lane(table[take, at])],
                    tiles[table[first, at]],
                    (((1,), (contract,)), ((), ())),
                    preferred_element_type=jnp.float32,
                )
            )
        for u in range(4):
            out[:, lane(table[give, i * 4 + u] + offset)] += products[u]
        return unused

    lax.fori_loop(0, table[6, first], step, 0)


def fetch_tiles(room, sources, target, sems):
    copies = [
        pltpu.make_async_copy(source, target.at[pl.ds(far * room + first, size)], sems.at[i])
        for i, ((far, first, size), source) in enumerate(zip(pieces(room), sources))
    ]
    for copy in copies:
        copy.start()
    target[SIDE * room] = jnp.zeros((BLK, BLK), jnp.bfloat16)
    return copies


SUM_PARTS = (
    (0, 0, 0, 0), (0, 1, 0, 1), (1, 0, 2, 0), (1, 1, 1, 1), (2, 0, 2, 1), (2, 1, 3, 0), (3, 0, 1, 0), (3, 1, 3, 1),
)


def term_parts(room):
    half = room // 2
    return (
        (0, 0, 0, room),
        (1, 0, 2 * room, half),
        (1, half, room + half, half),
        (2, 0, 2 * room + half, half),
        (2, half, 3 * room, half),
        (3, 0, room, half),
        (4, 0, 3 * room + half, half),
    )


def main_kernel(room, place, table, acts_in, grads_in, *refs):
    ups, downs = refs[:5], refs[5:10]
    keep_outs, send_out, up_outs, down_outs = refs[10:14], refs[14], refs[15:20], refs[20:25]
    acts, grads, up_tiles, down_tiles, sums, activated, hidden_grad, shares, sems = refs[25:]
    load_acts = pltpu.make_async_copy(acts_in, acts, sems.at[2, 0])
    load_grads = pltpu.make_async_copy(grads_in, grads, sems.at[2, 1])
    up_copies = fetch_tiles(room, ups, up_tiles, sems.at[0])
    load_acts.start()
    down_copies = fetch_tiles(room, downs, down_tiles, sems.at[1])
    load_grads.start()
    sums[...] = jnp.zeros_like(sums)
    for copy in up_copies:
        copy.wait()
    load_acts.wait()
    columns = activated.shape[1] // BLK
    block_products(table, 0, 1, 2, acts, up_tiles, sums, 0)
    for copy in down_copies:
        copy.wait()
    load_grads.wait()
    block_products(table, 3, 5, 4, grads, down_tiles, sums, 1, columns)

    def bend(i, unused):
        value, slope = gelu_parts(sums[:, lane(i)])
        activated[:, lane(i)] = value.astype(jnp.bfloat16)
        hidden_grad[:, lane(i)] = (sums[:, lane(i + columns)] * slope).astype(jnp.bfloat16)
        zero = jnp.zeros((sums.shape[0], BLK), jnp.float32)
        sums[:, lane(i)] = zero
        sums[:, lane(i + columns)] = zero
        return unused

    lax.fori_loop(0, columns, bend, 0)
    block_products(table, 0, 2, 1, hidden_grad, up_tiles, sums, 1)
    share = shares.shape[2] // BLK
    rows = shares.shape[1] // 2
    copies = []
    for first, core in ((SIDE, 1 - place[3]), (0, place[3])):
        for buffer, part, far, tokens in SUM_PARTS:
            base = (back(place[2], far) * 2 + core) * share

            def round_one(i, unused, base=base, at=first + buffer, part=part, tokens=tokens):
                shares[at, part * rows:(part + 1) * rows, lane(i)] = sums[
                    tokens * rows:(tokens + 1) * rows, lane(base + i)
                ].astype(jnp.bfloat16)
                return unused

            lax.fori_loop(0, share, round_one, 0)
        if first:
            copies.append(pltpu.make_async_copy(shares.at[pl.ds(SIDE, SIDE)], send_out, sems.at[2, 2]))
            copies[-1].start()
        else:
            for i in range(SIDE):
                copies.append(pltpu.make_async_copy(shares.at[i], keep_outs[i], sems.at[2, 3 + i]))
                copies[-1].start()
    for which, (left, right, terms, outs) in enumerate(
        ((acts, hidden_grad, up_tiles, up_outs), (activated, grads, down_tiles, down_outs))
    ):
        first = which * 3

        def body(i, unused, first=first, left=left, right=right, terms=terms):
            for u in range(4):
                at = i * 4 + u
                terms[table[first, at]] = lax.dot_general(
                    left[:, lane(table[first + 1, at])],
                    right[:, lane(table[first + 2, at])],
                    (((0,), (0,)), ((), ())),
                    preferred_element_type=jnp.float32,
                ).astype(jnp.bfloat16)
            return unused

        lax.fori_loop(0, table[6, first], body, 0)
        for i, (out, to, start, size) in enumerate(term_parts(room)):
            copies.append(
                pltpu.make_async_copy(
                    terms.at[pl.ds(start, size)], outs[out].at[pl.ds(to, size)], sems.at[which, i]
                )
            )
            copies[-1].start()
    for copy in copies:
        copy.wait()


def unpack_kernel(room, place, up_count, down_count, *refs):
    y, x = place[0], place[1]
    half = room // 2
    for owner_of, count, ins, outs in (
        (up_owner, up_count, refs[:5], refs[10:15]),
        (down_owner, down_count, refs[5:10], refs[15:20]),
    ):
        own, from_fore, from_back, rest_fore, rest_back = ins
        position = 0
        for out, to, start, size in sorted(term_parts(CAP), key=lambda part: part[2]):
            near, start = start // CAP, start % CAP
            live = jnp.clip(count[owner_of(y, x, 0, near)] - start, 0, size)
            live = jnp.minimum(live, room - position)
            low = jnp.clip(half - position, 0, live)

            def put_low(j, at, out=outs[out], to=to, own=own, first=rest_fore, second=from_back):
                out[to + j] = add(own[at], first[at], second[half + at])
                return at + 1

            def put_high(j, at, out=outs[out], to=to, own=own, first=from_fore, second=rest_back):
                out[to + j] = add(own[at], first[at], second[at - half])
                return at + 1

            position = lax.fori_loop(0, low, put_low, position)
            position = lax.fori_loop(low, live, put_high, position)


def finish_kernel(place, up_count, down_count, up_factor, down_factor, *refs):
    owner = place[0] * SIDE + place[1]
    half = CAP // 2
    for count, factor, ins, out in (
        (up_count, up_factor, refs[:5], refs[10]),
        (down_count, down_factor, refs[5:10], refs[11]),
    ):
        own, from_fore, from_back, rest_fore, rest_back = ins
        live = count[owner]
        for j in range(CAP):
            if j < half:
                items = (own[j], rest_fore[j], from_back[half + j])
            else:
                items = (own[j], from_fore[j], rest_back[j - half])
            total = sum(item.astype(jnp.float32) for item in items) * factor[j]
            out[j] = jnp.where(j < live, total, 0.0).astype(jnp.bfloat16)


def gather_far(room, place, up_count, down_count, near_up, near_down, flag=None):
    def kernel(*refs):
        pack_kernel(room, *refs)

    packed_up, packed_down = call(
        kernel, [blocks(room)] * 2, [S] * 3 + [V] * 10, [V] * 2, [], "pack", 3
    )(place, up_count, down_count, *near_up, *near_down)
    if flag is not None:
        flag, packed_up, packed_down = lax.optimization_barrier((flag, packed_up, packed_down))
    return spread([(packed_up, over_y), (packed_down, over_x)], flag)


def layer(room, place, table, far_up, far_down, activations, output_grad, up_factor, down_factor, up_count, down_count):
    tokens, width = activations.shape
    hidden_width = FF // lax.axis_size("tensor")
    share = width // (2 * SIDE)
    tiles = pltpu.VMEM((SIDE * room + 1, BLK, BLK), jnp.bfloat16)
    parts = [blocks(room)] * 3 + [blocks(room // 2)] * 2

    def main(*refs):
        main_kernel(room, *refs)

    def unpack(*refs):
        unpack_kernel(room, *refs)

    *keeps, send, up0, up1, up2, up3, up4, down0, down1, down2, down3, down4 = call(
        main,
        [jax.ShapeDtypeStruct((tokens, share), jnp.bfloat16)] * SIDE
        + [jax.ShapeDtypeStruct((SIDE, tokens, share), jnp.bfloat16)]
        + parts * 2,
        [S, S] + [A] * 12,
        [A] * 15,
        [pltpu.VMEM((tokens, width), jnp.bfloat16)] * 2
        + [tiles, tiles, pltpu.VMEM((tokens, 2 * hidden_width), jnp.float32)]
        + [pltpu.VMEM((tokens, hidden_width), jnp.bfloat16)] * 2
        + [pltpu.VMEM((2 * SIDE, tokens, share), jnp.bfloat16), pltpu.SemaphoreType.DMA((3, 8))],
        "main", 40,
    )(place, table, activations, output_grad, *far_up, *far_down)
    other = lax.ppermute(send, "tensor", [(t, t ^ 1) for t in range(2 * SIDE)])
    far_up_terms, far_down_terms = collect(
        [(up0, up1, up2, up3, up4, over_y), (down0, down1, down2, down3, down4, over_x)]
    )
    rows = tokens // 2
    from_fore = over_z(add(keeps[1], other[1]), 3)
    from_back = over_z(add(keeps[2], other[2]), 1)
    rest_fore = over_z(add(keeps[3][:rows], other[3][:rows], from_fore[:rows]), 3)
    rest_back = over_z(add(keeps[3][rows:], other[3][rows:], from_back[:rows]), 1)
    input_grad = jnp.concatenate(
        [
            add(keeps[0][:rows], other[0][:rows], rest_fore, from_back[rows:]),
            add(keeps[0][rows:], other[0][rows:], from_fore[rows:], rest_back),
        ]
    )
    caps = [blocks(CAP)] * 3 + [blocks(CAP // 2)] * 2
    sums = call(
        unpack, caps * 2, [S] * 3 + [V] * 10, [V] * 10, [], "unpack", 4
    )(place, up_count, down_count, *far_up_terms, *far_down_terms)
    near_up, near_down = collect([(*sums[:5], over_x), (*sums[5:], over_y)])
    up_grad, down_grad = call(
        finish_kernel, [blocks(CAP)] * 2, [S] * 5 + [V] * 10, [V] * 2, [], "finish", 3
    )(place, up_count, down_count, up_factor, down_factor, *near_up, *near_down)
    return input_grad, up_grad[None], down_grad[None]


def on_device(
    activations,
    output_grad,
    up_blocks,
    up_scale,
    down_blocks,
    down_scale,
    up_row_block,
    up_col_block,
    down_row_block,
    down_col_block,
    up_count,
    down_count,
):
    me, shard = lax.axis_index("fsdp"), lax.axis_index("tensor")
    place = jnp.stack([me // SIDE, me % SIDE, shard // 2, shard % 2]).astype(jnp.int32)
    up_count, down_count = up_count[0], down_count[0]
    names = (up_count, up_row_block[0], up_col_block[0], down_count, down_row_block[0], down_col_block[0])
    grad_norm = float(activations.shape[0] * lax.axis_size("fsdp")) ** (-0.5)
    rest = (
        activations,
        output_grad,
        up_scale[0].astype(jnp.float32) * grad_norm,
        down_scale[0].astype(jnp.float32) * grad_norm,
        up_count,
        down_count,
    )
    scaled_up = up_blocks[0] * up_scale[0][:, None, None]
    scaled_down = down_blocks[0] * down_scale[0][:, None, None]
    near_up, near_down = spread([(scaled_up, over_x), (scaled_down, over_y)])
    table, most = make_table(ROOM, place, *names)
    (far_up, far_down), most = gather_far(ROOM, place, up_count, down_count, near_up, near_down, most)
    crowded = most[0] > ROOM
    results = layer(ROOM, place, table, far_up, far_down, *rest)

    def full(results, near_up, near_down, *rest):
        room = SIDE * CAP
        far_up, far_down = gather_far(room, place, up_count, down_count, near_up, near_down)
        return layer(room, place, make_table(room, place, *names)[0], far_up, far_down, *rest)

    return lax.cond(
        crowded, full, lambda results, *unused: results, results, near_up, near_down, *rest
    )


def solution(mesh):
    return jax.shard_map(
        on_device,
        mesh=mesh,
        in_specs=(
            P("fsdp", None),
            P("fsdp", None),
            P("tensor", "fsdp", None, None),
            P("tensor", "fsdp"),
            P("tensor", "fsdp", None, None),
            P("tensor", "fsdp"),
            P("tensor", None),
            P("tensor", None),
            P("tensor", None),
            P("tensor", None),
            P("tensor", None),
            P("tensor", None),
        ),
        out_specs=(
            P("fsdp", "tensor"),
            P("tensor", "fsdp", None, None),
            P("tensor", "fsdp", None, None),
        ),
        check_vma=False,
    )
```

```python
import jax
import jax.numpy as jnp
from jax import lax
from jax.experimental import pallas as pl
from jax.experimental.pallas import tpu as pltpu
from jax.sharding import PartitionSpec as P

FF = 57344


ROOT_TWO_PI = 0.7978845608028654
CUBIC = 0.044715


def gelu_parts(hidden):
    square = hidden * hidden
    part = 0.5 + 0.5 * jnp.tanh(hidden * (ROOT_TWO_PI + (ROOT_TWO_PI * CUBIC) * square))
    twice = hidden * (2.0 * ROOT_TWO_PI + (6.0 * ROOT_TWO_PI * CUBIC) * square)
    return hidden * part, part + part * (1.0 - part) * twice


SIDE = 4
CAP = 12
BLK = 128
ROOM = 30
LIST = 192
V, S, A = pltpu.VMEM, pltpu.SMEM, pl.ANY


def shift_x(step):
    return [(y * SIDE + x, y * SIDE + (x + step) % SIDE) for y in range(SIDE) for x in range(SIDE)]


def shift_y(step):
    return [(y * SIDE + x, (y + step) % SIDE * SIDE + x) for y in range(SIDE) for x in range(SIDE)]


def shift_z(step):
    return [(z * 2 + c, (z + step) % SIDE * 2 + c) for z in range(SIDE) for c in range(2)]


def along(axis, shift):
    return lambda array, step: lax.ppermute(array, axis, shift(step))


over_x, over_y, over_z = along("fsdp", shift_x), along("fsdp", shift_y), along("tensor", shift_z)


def back(place, step):
    return lax.rem(place + SIDE - step, SIDE)


def any_tensor(flag):
    def moved(pairs):
        return lax.ppermute(flag, "tensor", pairs)

    flag = jnp.maximum(flag, moved([(t, t ^ 1) for t in range(8)]))
    flag = jnp.maximum(flag, moved([(t, (t + 2) % 8) for t in range(8)]))
    return jnp.maximum(flag, moved([(t, (t + 4) % 8) for t in range(8)]))


def spread(rings, flag=None, held=None):
    half = rings[0][0].shape[0] // 2
    first = [(move(own, 1), move(own, 3)) for own, move in rings]
    if flag is not None:
        first, flag = lax.optimization_barrier((first, any_tensor(flag)))
    if held is not None:
        first, held = lax.optimization_barrier((first, held))
    second = [
        (move(one[:half], 1), move(three[half:], 3))
        for (own, move), (one, three) in zip(rings, first)
    ]
    spreads = [
        (own, one, low, high, three)
        for (own, move), (one, three), (low, high) in zip(rings, first, second)
    ]
    return spreads if flag is None and held is None else (spreads, flag if held is None else held)


def add(*arrays):
    return sum(a.astype(jnp.float32) for a in arrays).astype(jnp.bfloat16)


def collect(rings):
    half = rings[0][3].shape[0]
    first = [(move(back, 3), move(fore, 1)) for own, back, fore, one, three, move in rings]
    second = [
        (move(add(one, from_fore[:half]), 3), move(add(three, from_back[:half]), 1))
        for (own, back, fore, one, three, move), (from_fore, from_back) in zip(rings, first)
    ]
    return [(ring[0],) + f + s for ring, f, s in zip(rings, first, second)]


def up_owner(y, x, far, near):
    return back(y, far) * SIDE + back(x, near)


def down_owner(y, x, far, near):
    return back(y, near) * SIDE + back(x, far)


def cost(us):
    return pl.CostEstimate(flops=0, bytes_accessed=int(us * 3e6), transcendentals=0)


def call(kernel, outs, in_spaces, out_spaces, scratch, name, us, limit=38):
    return pl.pallas_call(
        kernel,
        out_shape=outs,
        in_specs=[pl.BlockSpec(memory_space=s) for s in in_spaces],
        out_specs=[pl.BlockSpec(memory_space=s) for s in out_spaces],
        scratch_shapes=scratch,
        compiler_params=pltpu.CompilerParams(vmem_limit_bytes=limit * 1024 * 1024),
        cost_estimate=cost(us),
        name=name,
    )


def blocks(count):
    return jax.ShapeDtypeStruct((count, BLK, BLK), jnp.bfloat16)


def pieces(size):
    half = size // 2
    return ((0, 0, size), (1, 0, size), (2, 0, half), (2, half, half), (3, 0, size))


def pack_kernel(room, place, up_count, down_count, *refs):
    y, x = place[0], place[1]
    for owner_of, count, ins, out in (
        (up_owner, up_count, refs[:5], refs[10]),
        (down_owner, down_count, refs[5:10], refs[11]),
    ):
        position = 0
        for (near, first, size), source in zip(pieces(CAP), ins):
            live = jnp.clip(count[owner_of(y, x, 0, near)] - first, 0, size)
            live = jnp.minimum(live, room - position)

            def put(j, at, source=source, out=out):
                out[at] = source[j]
                return at + 1

            position = lax.fori_loop(0, live, put, position)


def table_kernel(room, place, up_count, up_row, up_col, down_count, down_row, down_col, table, most):
    y, x = place[0], place[1]
    largest = 0
    for first, owner_of, count, rows, cols in (
        (0, up_owner, up_count, up_row, up_col),
        (3, down_owner, down_count, down_row, down_col),
    ):
        def blank(i, unused, first=first):
            table[first, i] = SIDE * room
            table[first + 1, i] = 0
            table[first + 2, i] = 0
            return unused

        total = 0
        for far in range(SIDE):
            position = far * room
            wanted = 0
            for near in range(SIDE):
                owner = owner_of(y, x, far, near)
                wanted = wanted + count[owner]
                live = jnp.minimum(count[owner], (far + 1) * room - position)

                def note(j, unused, first=first, rows=rows, cols=cols, owner=owner, total=total, position=position):
                    table[first, total + j] = position + j
                    table[first + 1, total + j] = rows[owner * CAP + j]
                    table[first + 2, total + j] = cols[owner * CAP + j]
                    return unused

                lax.fori_loop(0, live, note, 0)
                total = total + live
                position = position + live
            largest = jnp.maximum(largest, wanted)
        padded = (total + 3) // 4
        lax.fori_loop(total, padded * 4, blank, 0)
        table[6, first] = padded
    most[0] = largest


def make_table(room, place, up_count, up_row, up_col, down_count, down_row, down_col, held=()):
    def kernel(*refs):
        table_kernel(room, *refs[:7], *refs[7 + len(held):])

    outs = [jax.ShapeDtypeStruct((8, LIST), jnp.int32), jax.ShapeDtypeStruct((1,), jnp.int32)]
    return call(kernel, outs, [S] * 7 + [V] * len(held), [S] * 2, [], "table", 3)(
        place, up_count, up_row, up_col, down_count, down_row, down_col, *held
    )


def lane(index):
    return pl.ds(pl.multiple_of(index * BLK, BLK), BLK)


def in_groups(groups, run):
    def twelve(i, unused):
        run(i * 12, 12)
        return unused

    def four(i, unused):
        run(i * 4, 4)
        return unused

    lax.fori_loop(0, groups // 3, twelve, 0)
    lax.fori_loop(groups // 3 * 3, groups, four, 0)


def block_products(table, first, take, give, left, tiles, out, contract, offset=0):
    def run(start, count):
        products = [
            lax.dot_general(
                left[:, lane(table[take, start + u])],
                tiles[table[first, start + u]],
                (((1,), (contract,)), ((), ())),
                preferred_element_type=jnp.float32,
            )
            for u in range(count)
        ]
        for u in range(count):
            out[:, lane(table[give, start + u] + offset)] += products[u]

    in_groups(table[6, first], run)


def fetch_tiles(room, sources, target, sems):
    copies = [
        pltpu.make_async_copy(source, target.at[pl.ds(far * room + first, size)], sems.at[i])
        for i, ((far, first, size), source) in enumerate(zip(pieces(room), sources))
    ]
    for copy in copies:
        copy.start()
    target[SIDE * room] = jnp.zeros((BLK, BLK), jnp.bfloat16)
    return copies


def term_parts(room):
    half = room // 2
    return (
        (0, 0, 0, room),
        (1, 0, 2 * room, half),
        (1, half, room + half, half),
        (2, 0, 2 * room + half, half),
        (2, half, 3 * room, half),
        (3, 0, room, half),
        (4, 0, 3 * room + half, half),
    )


def main_kernel(room, place, table, acts, grads, *refs):
    ups, downs = refs[:5], refs[5:10]
    partial_out, up_outs, down_outs = refs[10], refs[11:16], refs[16:21]
    up_tiles, down_tiles, sums, activated, hidden_grad, shares, sems = refs[21:]
    up_copies = fetch_tiles(room, ups, up_tiles, sems.at[0])
    down_copies = fetch_tiles(room, downs, down_tiles, sems.at[1])
    sums[...] = jnp.zeros_like(sums)
    for copy in up_copies:
        copy.wait()
    columns = activated.shape[1] // BLK
    block_products(table, 0, 1, 2, acts, up_tiles, sums, 0)
    for copy in down_copies:
        copy.wait()
    block_products(table, 3, 5, 4, grads, down_tiles, sums, 1, columns)

    def bend(i, unused):
        for row in range(0, sums.shape[0], 64):
            rows = slice(row, row + 64)
            value, slope = gelu_parts(sums[rows, lane(i)])
            activated[rows, lane(i)] = value.astype(jnp.bfloat16)
            hidden_grad[rows, lane(i)] = (sums[rows, lane(i + columns)] * slope).astype(jnp.bfloat16)
        zero = jnp.zeros((sums.shape[0], BLK), jnp.float32)
        sums[:, lane(i)] = zero
        sums[:, lane(i + columns)] = zero
        return unused

    lax.fori_loop(0, columns, bend, 0)
    block_products(table, 0, 2, 1, hidden_grad, up_tiles, sums, 1)
    def round_two(i, unused):
        at = pl.ds(pl.multiple_of(i * 2 * BLK, BLK), 2 * BLK)
        shares[:, at] = sums[:, at].astype(jnp.bfloat16)
        return unused

    lax.fori_loop(0, columns, round_two, 0)
    copies = [pltpu.make_async_copy(shares, partial_out, sems.at[2, 2])]
    copies[0].start()
    for which, (left, right, terms, outs) in enumerate(
        ((acts, hidden_grad, up_tiles, up_outs), (activated, grads, down_tiles, down_outs))
    ):
        first = which * 3

        def run(start, count, first=first, left=left, right=right, terms=terms):
            for at in range(count):
                at = start + at
                terms[table[first, at]] = lax.dot_general(
                    left[:, lane(table[first + 1, at])],
                    right[:, lane(table[first + 2, at])],
                    (((0,), (0,)), ((), ())),
                    preferred_element_type=jnp.float32,
                ).astype(jnp.bfloat16)

        in_groups(table[6, first], run)
        for i, (out, to, start, size) in enumerate(term_parts(room)):
            copies.append(
                pltpu.make_async_copy(
                    terms.at[pl.ds(start, size)], outs[out].at[pl.ds(to, size)], sems.at[which, i]
                )
            )
            copies[-1].start()
    for copy in copies:
        copy.wait()


def unpack_kernel(room, place, up_count, down_count, *refs):
    y, x = place[0], place[1]
    half = room // 2
    for owner_of, count, ins, outs in (
        (up_owner, up_count, refs[:5], refs[10:15]),
        (down_owner, down_count, refs[5:10], refs[15:20]),
    ):
        own, from_fore, from_back, rest_fore, rest_back = ins
        position = 0
        for out, to, start, size in sorted(term_parts(CAP), key=lambda part: part[2]):
            near, start = start // CAP, start % CAP
            live = jnp.clip(count[owner_of(y, x, 0, near)] - start, 0, size)
            live = jnp.minimum(live, room - position)
            low = jnp.clip(half - position, 0, live)

            def put_low(j, at, out=outs[out], to=to, own=own, first=rest_fore, second=from_back):
                out[to + j] = add(own[at], first[at], second[half + at])
                return at + 1

            def put_high(j, at, out=outs[out], to=to, own=own, first=from_fore, second=rest_back):
                out[to + j] = add(own[at], first[at], second[at - half])
                return at + 1

            position = lax.fori_loop(0, low, put_low, position)
            position = lax.fori_loop(low, live, put_high, position)


def finish_kernel(place, up_count, down_count, up_factor, down_factor, *refs):
    owner = place[0] * SIDE + place[1]
    half = CAP // 2
    for count, factor, ins, out in (
        (up_count, up_factor, refs[:5], refs[10]),
        (down_count, down_factor, refs[5:10], refs[11]),
    ):
        own, from_fore, from_back, rest_fore, rest_back = ins
        live = count[owner]
        for j in range(CAP):
            if j < half:
                items = (own[j], rest_fore[j], from_back[half + j])
            else:
                items = (own[j], from_fore[j], rest_back[j - half])
            total = sum(item.astype(jnp.float32) for item in items) * factor[j]
            out[j] = jnp.where(j < live, total, 0.0).astype(jnp.bfloat16)


def gather_far(room, place, up_count, down_count, near_up, near_down, flag=None):
    def kernel(*refs):
        pack_kernel(room, *refs)

    packed_up, packed_down = call(
        kernel, [blocks(room)] * 2, [S] * 3 + [V] * 10, [V] * 2, [], "pack", 3
    )(place, up_count, down_count, *near_up, *near_down)
    if flag is not None:
        flag, packed_up, packed_down = lax.optimization_barrier((flag, packed_up, packed_down))
    return spread([(packed_up, over_y), (packed_down, over_x)], flag)


def layer(room, place, table, far_up, far_down, activations, output_grad, up_factor, down_factor, up_count, down_count):
    tokens, width = activations.shape
    hidden_width = FF // lax.axis_size("tensor")
    tiles = pltpu.VMEM((SIDE * room + 1, BLK, BLK), jnp.bfloat16)
    parts = [blocks(room)] * 3 + [blocks(room // 2)] * 2

    def main(*refs):
        main_kernel(room, *refs)

    def unpack(*refs):
        unpack_kernel(room, *refs)

    partial, up0, up1, up2, up3, up4, down0, down1, down2, down3, down4 = call(
        main,
        [jax.ShapeDtypeStruct((tokens, width), jnp.bfloat16)] + parts * 2,
        [S, S, V, V] + [A] * 10,
        [A] * 11,
        [tiles, tiles, pltpu.VMEM((tokens, 2 * hidden_width), jnp.float32)]
        + [pltpu.VMEM((tokens, hidden_width), jnp.bfloat16)] * 2
        + [pltpu.VMEM((tokens, width), jnp.bfloat16), pltpu.SemaphoreType.DMA((3, 8))],
        "main", 40, 38 if room == ROOM else 60,
    )(place, table, activations, output_grad, *far_up, *far_down)
    input_grad = lax.psum_scatter(partial, "tensor", scatter_dimension=1, tiled=True)
    far_up_terms, far_down_terms = collect(
        [(up0, up1, up2, up3, up4, over_y), (down0, down1, down2, down3, down4, over_x)]
    )
    caps = [blocks(CAP)] * 3 + [blocks(CAP // 2)] * 2
    sums = call(
        unpack, caps * 2, [S] * 3 + [V] * 10, [V] * 10, [], "unpack", 4
    )(place, up_count, down_count, *far_up_terms, *far_down_terms)
    near_up, near_down = collect([(*sums[:5], over_x), (*sums[5:], over_y)])
    up_grad, down_grad = call(
        finish_kernel, [blocks(CAP)] * 2, [S] * 5 + [V] * 10, [V] * 2, [], "finish", 3
    )(place, up_count, down_count, up_factor, down_factor, *near_up, *near_down)
    return input_grad, up_grad[None], down_grad[None]


def on_device(
    activations,
    output_grad,
    up_blocks,
    up_scale,
    down_blocks,
    down_scale,
    up_row_block,
    up_col_block,
    down_row_block,
    down_col_block,
    up_count,
    down_count,
):
    me, shard = lax.axis_index("fsdp"), lax.axis_index("tensor")
    place = jnp.stack([me // SIDE, me % SIDE, shard // 2, shard % 2]).astype(jnp.int32)
    up_count, down_count = up_count[0], down_count[0]
    names = (up_count, up_row_block[0], up_col_block[0], down_count, down_row_block[0], down_col_block[0])
    grad_norm = float(activations.shape[0] * lax.axis_size("fsdp")) ** (-0.5)
    wide = (activations, output_grad)
    rest = (
        up_scale[0].astype(jnp.float32) * grad_norm,
        down_scale[0].astype(jnp.float32) * grad_norm,
        up_count,
        down_count,
    )
    scaled_up = up_blocks[0] * up_scale[0][:, None, None]
    scaled_down = down_blocks[0] * down_scale[0][:, None, None]
    activations = pltpu.with_memory_space_constraint(activations, pltpu.VMEM)
    output_grad = pltpu.with_memory_space_constraint(output_grad, pltpu.VMEM)
    table, most = make_table(ROOM, place, *names, held=(activations, output_grad))
    (near_up, near_down), (table, most) = spread(
        [(scaled_up, over_x), (scaled_down, over_y)], held=(table, most)
    )
    (far_up, far_down), most = gather_far(ROOM, place, up_count, down_count, near_up, near_down, most)
    crowded = most[0] > ROOM
    results = layer(ROOM, place, table, far_up, far_down, activations, output_grad, *rest)

    def full(results, near_up, near_down, *rest):
        room = SIDE * CAP
        far_up, far_down = gather_far(room, place, up_count, down_count, near_up, near_down)
        return layer(room, place, make_table(room, place, *names)[0], far_up, far_down, *rest)

    return lax.cond(
        crowded, full, lambda results, *unused: results, results, near_up, near_down, wide[0], wide[1], *rest
    )


def solution(mesh):
    return jax.shard_map(
        on_device,
        mesh=mesh,
        in_specs=(
            P("fsdp", None),
            P("fsdp", None),
            P("tensor", "fsdp", None, None),
            P("tensor", "fsdp"),
            P("tensor", "fsdp", None, None),
            P("tensor", "fsdp"),
            P("tensor", None),
            P("tensor", None),
            P("tensor", None),
            P("tensor", None),
            P("tensor", None),
            P("tensor", None),
        ),
        out_specs=(
            P("fsdp", "tensor"),
            P("tensor", "fsdp", None, None),
            P("tensor", "fsdp", None, None),
        ),
        check_vma=False,
    )
```

```python
import jax
import jax.numpy as jnp
from jax import lax
from jax.experimental import pallas as pl
from jax.experimental.pallas import tpu as pltpu
from jax.sharding import PartitionSpec as P

FF = 57344


ROOT_TWO_PI = 0.7978845608028654
CUBIC = 0.044715


def gelu_parts(hidden):
    square = hidden * hidden
    part = 0.5 + 0.5 * jnp.tanh(hidden * (ROOT_TWO_PI + (ROOT_TWO_PI * CUBIC) * square))
    twice = hidden * (2.0 * ROOT_TWO_PI + (6.0 * ROOT_TWO_PI * CUBIC) * square)
    return hidden * part, part + part * (1.0 - part) * twice


SIDE = 4
CAP = 12
BLK = 128
ROOM = 30
LIST = 192
V, S, A = pltpu.VMEM, pltpu.SMEM, pl.ANY


def shift_x(step):
    return [(y * SIDE + x, y * SIDE + (x + step) % SIDE) for y in range(SIDE) for x in range(SIDE)]


def shift_y(step):
    return [(y * SIDE + x, (y + step) % SIDE * SIDE + x) for y in range(SIDE) for x in range(SIDE)]


def shift_z(step):
    return [(z * 2 + c, (z + step) % SIDE * 2 + c) for z in range(SIDE) for c in range(2)]


def along(axis, shift):
    return lambda array, step: lax.ppermute(array, axis, shift(step))


over_x, over_y, over_z = along("fsdp", shift_x), along("fsdp", shift_y), along("tensor", shift_z)


def back(place, step):
    return lax.rem(place + SIDE - step, SIDE)


def any_tensor(flag):
    def moved(pairs):
        return lax.ppermute(flag, "tensor", pairs)

    flag = jnp.maximum(flag, moved([(t, t ^ 1) for t in range(8)]))
    flag = jnp.maximum(flag, moved([(t, (t + 2) % 8) for t in range(8)]))
    return jnp.maximum(flag, moved([(t, (t + 4) % 8) for t in range(8)]))


def spread(rings, flag=None, held=None):
    half = rings[0][0].shape[0] // 2
    first = [(move(own, 1), move(own, 3)) for own, move in rings]
    if flag is not None:
        first, flag = lax.optimization_barrier((first, any_tensor(flag)))
    if held is not None:
        first, held = lax.optimization_barrier((first, held))
    second = [
        (move(one[:half], 1), move(three[half:], 3))
        for (own, move), (one, three) in zip(rings, first)
    ]
    spreads = [
        (own, one, low, high, three)
        for (own, move), (one, three), (low, high) in zip(rings, first, second)
    ]
    return spreads if flag is None and held is None else (spreads, flag if held is None else held)


def add(*arrays):
    return sum(a.astype(jnp.float32) for a in arrays).astype(jnp.bfloat16)


def collect(rings):
    half = rings[0][3].shape[0]
    first = [(move(back, 3), move(fore, 1)) for own, back, fore, one, three, move in rings]
    second = [
        (move(add(one, from_fore[:half]), 3), move(add(three, from_back[:half]), 1))
        for (own, back, fore, one, three, move), (from_fore, from_back) in zip(rings, first)
    ]
    return [(ring[0],) + f + s for ring, f, s in zip(rings, first, second)]


def up_owner(y, x, far, near):
    return back(y, far) * SIDE + back(x, near)


def down_owner(y, x, far, near):
    return back(y, near) * SIDE + back(x, far)


def cost(us):
    return pl.CostEstimate(flops=0, bytes_accessed=int(us * 3e6), transcendentals=0)


def call(kernel, outs, in_spaces, out_spaces, scratch, name, us, limit=38):
    return pl.pallas_call(
        kernel,
        out_shape=outs,
        in_specs=[pl.BlockSpec(memory_space=s) for s in in_spaces],
        out_specs=[pl.BlockSpec(memory_space=s) for s in out_spaces],
        scratch_shapes=scratch,
        compiler_params=pltpu.CompilerParams(vmem_limit_bytes=limit * 1024 * 1024),
        cost_estimate=cost(us),
        name=name,
    )


def blocks(count):
    return jax.ShapeDtypeStruct((count, BLK, BLK), jnp.bfloat16)


def pieces(size):
    half = size // 2
    return ((0, 0, size), (1, 0, size), (2, 0, half), (2, half, half), (3, 0, size))


def pack_kernel(room, place, up_count, down_count, *refs):
    y, x = place[0], place[1]
    for owner_of, count, ins, out in (
        (up_owner, up_count, refs[:5], refs[10]),
        (down_owner, down_count, refs[5:10], refs[11]),
    ):
        position = 0
        for (near, first, size), source in zip(pieces(CAP), ins):
            live = jnp.clip(count[owner_of(y, x, 0, near)] - first, 0, size)
            live = jnp.minimum(live, room - position)

            def put(j, at, source=source, out=out):
                out[at] = source[j]
                return at + 1

            position = lax.fori_loop(0, live, put, position)


def table_kernel(room, place, up_count, up_row, up_col, down_count, down_row, down_col, table):
    y, x = place[0], place[1]
    for first, owner_of, count, rows, cols in (
        (0, up_owner, up_count, up_row, up_col),
        (3, down_owner, down_count, down_row, down_col),
    ):
        def blank(i, unused, first=first):
            table[first, i] = SIDE * room
            table[first + 1, i] = 0
            table[first + 2, i] = 0
            return unused

        total = 0
        for far in range(SIDE):
            position = far * room
            for near in range(SIDE):
                owner = owner_of(y, x, far, near)
                live = jnp.minimum(count[owner], (far + 1) * room - position)

                def note(j, unused, first=first, rows=rows, cols=cols, owner=owner, total=total, position=position):
                    table[first, total + j] = position + j
                    table[first + 1, total + j] = rows[owner * CAP + j]
                    table[first + 2, total + j] = cols[owner * CAP + j]
                    return unused

                lax.fori_loop(0, live, note, 0)
                total = total + live
                position = position + live
        padded = (total + 3) // 4
        lax.fori_loop(total, padded * 4, blank, 0)
        table[6, first] = padded


def make_table(room, place, up_count, up_row, up_col, down_count, down_row, down_col, held=()):
    def kernel(*refs):
        table_kernel(room, *refs[:7], refs[-1])

    outs = [jax.ShapeDtypeStruct((8, LIST), jnp.int32)]
    return call(kernel, outs, [S] * 7 + [V] * len(held), [S], [], "table", 3)(
        place, up_count, up_row, up_col, down_count, down_row, down_col, *held
    )[0]


def crowd_kernel(up_count, down_count, most):
    largest = 0
    for line in range(SIDE):
        largest = jnp.maximum(largest, sum(up_count[line * SIDE + i] for i in range(SIDE)))
        largest = jnp.maximum(largest, sum(down_count[i * SIDE + line] for i in range(SIDE)))
    most[0] = largest


def lane(index):
    return pl.ds(pl.multiple_of(index * BLK, BLK), BLK)


def in_groups(groups, run):
    def twelve(i, unused):
        run(i * 12, 12)
        return unused

    def four(i, unused):
        run(i * 4, 4)
        return unused

    lax.fori_loop(0, groups // 3, twelve, 0)
    lax.fori_loop(groups // 3 * 3, groups, four, 0)


def block_products(table, first, take, give, left, tiles, out, contract, offset=0):
    def run(start, count):
        products = [
            lax.dot_general(
                left[:, lane(table[take, start + u])],
                tiles[table[first, start + u]],
                (((1,), (contract,)), ((), ())),
                preferred_element_type=jnp.float32,
            )
            for u in range(count)
        ]
        for u in range(count):
            out[:, lane(table[give, start + u] + offset)] += products[u]

    in_groups(table[6, first], run)


def fetch_tiles(room, sources, target, sems):
    copies = [
        pltpu.make_async_copy(source, target.at[pl.ds(far * room + first, size)], sems.at[i])
        for i, ((far, first, size), source) in enumerate(zip(pieces(room), sources))
    ]
    for copy in copies:
        copy.start()
    target[SIDE * room] = jnp.zeros((BLK, BLK), jnp.bfloat16)
    return copies


def term_parts(room):
    half = room // 2
    return (
        (0, 0, 0, room),
        (1, 0, 2 * room, half),
        (1, half, room + half, half),
        (2, 0, 2 * room + half, half),
        (2, half, 3 * room, half),
        (3, 0, room, half),
        (4, 0, 3 * room + half, half),
    )


def main_kernel(room, place, table, acts, grads, *refs):
    ups, downs = refs[:5], refs[5:10]
    partial_out, up_outs, down_outs = refs[10], refs[11:16], refs[16:21]
    up_tiles, down_tiles, sums, activated, hidden_grad, shares, sems = refs[21:]
    up_copies = fetch_tiles(room, ups, up_tiles, sems.at[0])
    down_copies = fetch_tiles(room, downs, down_tiles, sems.at[1])
    sums[...] = jnp.zeros_like(sums)
    for copy in up_copies:
        copy.wait()
    columns = activated.shape[1] // BLK
    block_products(table, 0, 1, 2, acts, up_tiles, sums, 0)
    for copy in down_copies:
        copy.wait()
    block_products(table, 3, 5, 4, grads, down_tiles, sums, 1, columns)

    def bend(i, unused):
        for row in range(0, sums.shape[0], 64):
            rows = slice(row, row + 64)
            value, slope = gelu_parts(sums[rows, lane(i)])
            activated[rows, lane(i)] = value.astype(jnp.bfloat16)
            hidden_grad[rows, lane(i)] = (sums[rows, lane(i + columns)] * slope).astype(jnp.bfloat16)
        zero = jnp.zeros((sums.shape[0], BLK), jnp.float32)
        sums[:, lane(i)] = zero
        sums[:, lane(i + columns)] = zero
        return unused

    lax.fori_loop(0, columns, bend, 0)
    block_products(table, 0, 2, 1, hidden_grad, up_tiles, sums, 1)
    def round_two(i, unused):
        at = pl.ds(pl.multiple_of(i * 2 * BLK, BLK), 2 * BLK)
        shares[:, at] = sums[:, at].astype(jnp.bfloat16)
        return unused

    lax.fori_loop(0, columns, round_two, 0)
    copies = [pltpu.make_async_copy(shares, partial_out, sems.at[2, 2])]
    copies[0].start()
    for which, (left, right, terms, outs) in enumerate(
        ((acts, hidden_grad, up_tiles, up_outs), (activated, grads, down_tiles, down_outs))
    ):
        first = which * 3

        def run(start, count, first=first, left=left, right=right, terms=terms):
            for at in range(count):
                at = start + at
                terms[table[first, at]] = lax.dot_general(
                    left[:, lane(table[first + 1, at])],
                    right[:, lane(table[first + 2, at])],
                    (((0,), (0,)), ((), ())),
                    preferred_element_type=jnp.float32,
                ).astype(jnp.bfloat16)

        in_groups(table[6, first], run)
        for i, (out, to, start, size) in enumerate(term_parts(room)):
            copies.append(
                pltpu.make_async_copy(
                    terms.at[pl.ds(start, size)], outs[out].at[pl.ds(to, size)], sems.at[which, i]
                )
            )
            copies[-1].start()
    for copy in copies:
        copy.wait()


def unpack_kernel(room, place, up_count, down_count, *refs):
    y, x = place[0], place[1]
    half = room // 2
    for owner_of, count, ins, outs in (
        (up_owner, up_count, refs[:5], refs[10:15]),
        (down_owner, down_count, refs[5:10], refs[15:20]),
    ):
        own, from_fore, from_back, rest_fore, rest_back = ins
        position = 0
        for out, to, start, size in sorted(term_parts(CAP), key=lambda part: part[2]):
            near, start = start // CAP, start % CAP
            live = jnp.clip(count[owner_of(y, x, 0, near)] - start, 0, size)
            live = jnp.minimum(live, room - position)
            low = jnp.clip(half - position, 0, live)

            def put_low(j, at, out=outs[out], to=to, own=own, first=rest_fore, second=from_back):
                out[to + j] = add(own[at], first[at], second[half + at])
                return at + 1

            def put_high(j, at, out=outs[out], to=to, own=own, first=from_fore, second=rest_back):
                out[to + j] = add(own[at], first[at], second[at - half])
                return at + 1

            position = lax.fori_loop(0, low, put_low, position)
            position = lax.fori_loop(low, live, put_high, position)


def finish_kernel(place, up_count, down_count, up_factor, down_factor, *refs):
    owner = place[0] * SIDE + place[1]
    half = CAP // 2
    for count, factor, ins, out in (
        (up_count, up_factor, refs[:5], refs[10]),
        (down_count, down_factor, refs[5:10], refs[11]),
    ):
        own, from_fore, from_back, rest_fore, rest_back = ins
        live = count[owner]
        for j in range(CAP):
            if j < half:
                items = (own[j], rest_fore[j], from_back[half + j])
            else:
                items = (own[j], from_fore[j], rest_back[j - half])
            total = sum(item.astype(jnp.float32) for item in items) * factor[j]
            out[j] = jnp.where(j < live, total, 0.0).astype(jnp.bfloat16)


def gather_far(room, place, up_count, down_count, near_up, near_down, flag=None):
    def kernel(*refs):
        pack_kernel(room, *refs)

    packed_up, packed_down = call(
        kernel, [blocks(room)] * 2, [S] * 3 + [V] * 10, [V] * 2, [], "pack", 3
    )(place, up_count, down_count, *near_up, *near_down)
    if flag is not None:
        flag, packed_up, packed_down = lax.optimization_barrier((flag, packed_up, packed_down))
    return spread([(packed_up, over_y), (packed_down, over_x)], flag)


def layer(room, place, table, far_up, far_down, activations, output_grad, up_factor, down_factor, up_count, down_count):
    tokens, width = activations.shape
    hidden_width = FF // lax.axis_size("tensor")
    tiles = pltpu.VMEM((SIDE * room + 1, BLK, BLK), jnp.bfloat16)
    parts = [blocks(room)] * 3 + [blocks(room // 2)] * 2

    def main(*refs):
        main_kernel(room, *refs)

    def unpack(*refs):
        unpack_kernel(room, *refs)

    partial, up0, up1, up2, up3, up4, down0, down1, down2, down3, down4 = call(
        main,
        [jax.ShapeDtypeStruct((tokens, width), jnp.bfloat16)] + parts * 2,
        [S, S, V, V] + [A] * 10,
        [A] * 11,
        [tiles, tiles, pltpu.VMEM((tokens, 2 * hidden_width), jnp.float32)]
        + [pltpu.VMEM((tokens, hidden_width), jnp.bfloat16)] * 2
        + [pltpu.VMEM((tokens, width), jnp.bfloat16), pltpu.SemaphoreType.DMA((3, 8))],
        "main", 40, 38 if room == ROOM else 60,
    )(place, table, activations, output_grad, *far_up, *far_down)
    input_grad = lax.psum_scatter(partial, "tensor", scatter_dimension=1, tiled=True)
    far_up_terms, far_down_terms = collect(
        [(up0, up1, up2, up3, up4, over_y), (down0, down1, down2, down3, down4, over_x)]
    )
    caps = [blocks(CAP)] * 3 + [blocks(CAP // 2)] * 2
    sums = call(
        unpack, caps * 2, [S] * 3 + [V] * 10, [V] * 10, [], "unpack", 4
    )(place, up_count, down_count, *far_up_terms, *far_down_terms)
    near_up, near_down = collect([(*sums[:5], over_x), (*sums[5:], over_y)])
    up_grad, down_grad = call(
        finish_kernel, [blocks(CAP)] * 2, [S] * 5 + [V] * 10, [V] * 2, [], "finish", 3
    )(place, up_count, down_count, up_factor, down_factor, *near_up, *near_down)
    return input_grad, up_grad[None], down_grad[None]


def on_device(
    activations,
    output_grad,
    up_blocks,
    up_scale,
    down_blocks,
    down_scale,
    up_row_block,
    up_col_block,
    down_row_block,
    down_col_block,
    up_count,
    down_count,
):
    me, shard = lax.axis_index("fsdp"), lax.axis_index("tensor")
    place = jnp.stack([me // SIDE, me % SIDE, shard // 2, shard % 2]).astype(jnp.int32)
    up_count, down_count = up_count[0], down_count[0]
    names = (up_count, up_row_block[0], up_col_block[0], down_count, down_row_block[0], down_col_block[0])
    grad_norm = float(activations.shape[0] * lax.axis_size("fsdp")) ** (-0.5)
    wide = (activations, output_grad)
    rest = (
        up_scale[0].astype(jnp.float32) * grad_norm,
        down_scale[0].astype(jnp.float32) * grad_norm,
        up_count,
        down_count,
    )
    scaled_up = up_blocks[0] * up_scale[0][:, None, None]
    scaled_down = down_blocks[0] * down_scale[0][:, None, None]
    activations = pltpu.with_memory_space_constraint(activations, pltpu.VMEM)
    output_grad = pltpu.with_memory_space_constraint(output_grad, pltpu.VMEM)
    (most,) = call(
        crowd_kernel, [jax.ShapeDtypeStruct((1,), jnp.int32)], [S, S], [S], [], "crowd", 1
    )(up_count, down_count)
    near_up, near_down = spread([(scaled_up, over_x), (scaled_down, over_y)])
    (far_up, far_down), most = gather_far(ROOM, place, up_count, down_count, near_up, near_down, most)
    table = make_table(ROOM, place, *names, held=(activations, output_grad))
    crowded = most[0] > ROOM
    results = layer(ROOM, place, table, far_up, far_down, activations, output_grad, *rest)

    def full(results, near_up, near_down, *rest):
        room = SIDE * CAP
        far_up, far_down = gather_far(room, place, up_count, down_count, near_up, near_down)
        return layer(room, place, make_table(room, place, *names), far_up, far_down, *rest)

    return lax.cond(
        crowded, full, lambda results, *unused: results, results, near_up, near_down, wide[0], wide[1], *rest
    )


def solution(mesh):
    return jax.shard_map(
        on_device,
        mesh=mesh,
        in_specs=(
            P("fsdp", None),
            P("fsdp", None),
            P("tensor", "fsdp", None, None),
            P("tensor", "fsdp"),
            P("tensor", "fsdp", None, None),
            P("tensor", "fsdp"),
            P("tensor", None),
            P("tensor", None),
            P("tensor", None),
            P("tensor", None),
            P("tensor", None),
            P("tensor", None),
        ),
        out_specs=(
            P("fsdp", "tensor"),
            P("tensor", "fsdp", None, None),
            P("tensor", "fsdp", None, None),
        ),
        check_vma=False,
    )
```

```python
import jax
import jax.numpy as jnp
from jax import lax
from jax.experimental import pallas as pl
from jax.experimental.pallas import tpu as pltpu
from jax.sharding import PartitionSpec as P

FF = 57344


ROOT_TWO_PI = 0.7978845608028654
CUBIC = 0.044715


def gelu_parts(hidden):
    square = hidden * hidden
    part = 0.5 + 0.5 * jnp.tanh(hidden * (ROOT_TWO_PI + (ROOT_TWO_PI * CUBIC) * square))
    twice = hidden * (2.0 * ROOT_TWO_PI + (6.0 * ROOT_TWO_PI * CUBIC) * square)
    return hidden * part, part + part * (1.0 - part) * twice


SIDE = 4
CAP = 12
BLK = 128
ROOM = 30
LIST = 192
V, S, A = pltpu.VMEM, pltpu.SMEM, pl.ANY


def shift_x(step):
    return [(y * SIDE + x, y * SIDE + (x + step) % SIDE) for y in range(SIDE) for x in range(SIDE)]


def shift_y(step):
    return [(y * SIDE + x, (y + step) % SIDE * SIDE + x) for y in range(SIDE) for x in range(SIDE)]


def shift_z(step):
    return [(z * 2 + c, (z + step) % SIDE * 2 + c) for z in range(SIDE) for c in range(2)]


def along(axis, shift):
    return lambda array, step: lax.ppermute(array, axis, shift(step))


over_x, over_y, over_z = along("fsdp", shift_x), along("fsdp", shift_y), along("tensor", shift_z)


def back(place, step):
    return lax.rem(place + SIDE - step, SIDE)


def any_tensor(flag):
    def moved(pairs):
        return lax.ppermute(flag, "tensor", pairs)

    flag = jnp.maximum(flag, moved([(t, t ^ 1) for t in range(8)]))
    flag = jnp.maximum(flag, moved([(t, (t + 2) % 8) for t in range(8)]))
    return jnp.maximum(flag, moved([(t, (t + 4) % 8) for t in range(8)]))


def spread(rings, flag=None, held=None):
    half = rings[0][0].shape[0] // 2
    first = [(move(own, 1), move(own, 3)) for own, move in rings]
    if flag is not None:
        first, flag = lax.optimization_barrier((first, any_tensor(flag)))
    if held is not None:
        first, held = lax.optimization_barrier((first, held))
    second = [
        (move(one[:half], 1), move(three[half:], 3))
        for (own, move), (one, three) in zip(rings, first)
    ]
    spreads = [
        (own, one, low, high, three)
        for (own, move), (one, three), (low, high) in zip(rings, first, second)
    ]
    return spreads if flag is None and held is None else (spreads, flag if held is None else held)


def add(*arrays):
    return sum(a.astype(jnp.float32) for a in arrays).astype(jnp.bfloat16)


def collect(rings):
    half = rings[0][3].shape[0]
    first = [(move(back, 3), move(fore, 1)) for own, back, fore, one, three, move in rings]
    second = [
        (move(add(one, from_fore[:half]), 3), move(add(three, from_back[:half]), 1))
        for (own, back, fore, one, three, move), (from_fore, from_back) in zip(rings, first)
    ]
    return [(ring[0],) + f + s for ring, f, s in zip(rings, first, second)]


def up_owner(y, x, far, near):
    return back(y, far) * SIDE + back(x, near)


def down_owner(y, x, far, near):
    return back(y, near) * SIDE + back(x, far)


def cost(us):
    return pl.CostEstimate(flops=0, bytes_accessed=int(us * 3e6), transcendentals=0)


def call(kernel, outs, in_spaces, out_spaces, scratch, name, us, limit=38):
    return pl.pallas_call(
        kernel,
        out_shape=outs,
        in_specs=[pl.BlockSpec(memory_space=s) for s in in_spaces],
        out_specs=[pl.BlockSpec(memory_space=s) for s in out_spaces],
        scratch_shapes=scratch,
        compiler_params=pltpu.CompilerParams(vmem_limit_bytes=limit * 1024 * 1024),
        cost_estimate=cost(us),
        name=name,
    )


def blocks(count):
    return jax.ShapeDtypeStruct((count, BLK, BLK), jnp.bfloat16)


def pieces(size):
    half = size // 2
    return ((0, 0, size), (1, 0, size), (2, 0, half), (2, half, half), (3, 0, size))


def pack_kernel(room, place, up_count, down_count, *refs):
    y, x = place[0], place[1]
    for owner_of, count, ins, out in (
        (up_owner, up_count, refs[:5], refs[10]),
        (down_owner, down_count, refs[5:10], refs[11]),
    ):
        position = 0
        for (near, first, size), source in zip(pieces(CAP), ins):
            live = jnp.clip(count[owner_of(y, x, 0, near)] - first, 0, size)
            live = jnp.minimum(live, room - position)

            def put(j, at, source=source, out=out):
                out[at] = source[j]
                return at + 1

            position = lax.fori_loop(0, live, put, position)


def table_kernel(room, place, up_count, up_row, up_col, down_count, down_row, down_col, table, most):
    y, x = place[0], place[1]
    largest = 0
    for first, owner_of, count, rows, cols in (
        (0, up_owner, up_count, up_row, up_col),
        (3, down_owner, down_count, down_row, down_col),
    ):
        def blank(i, unused, first=first):
            table[first, i] = SIDE * room
            table[first + 1, i] = 0
            table[first + 2, i] = 0
            return unused

        total = 0
        for far in range(SIDE):
            position = far * room
            wanted = 0
            for near in range(SIDE):
                owner = owner_of(y, x, far, near)
                wanted = wanted + count[owner]
                live = jnp.minimum(count[owner], (far + 1) * room - position)

                def note(j, unused, first=first, rows=rows, cols=cols, owner=owner, total=total, position=position):
                    table[first, total + j] = position + j
                    table[first + 1, total + j] = rows[owner * CAP + j]
                    table[first + 2, total + j] = cols[owner * CAP + j]
                    return unused

                lax.fori_loop(0, live, note, 0)
                total = total + live
                position = position + live
            largest = jnp.maximum(largest, wanted)
        padded = (total + 3) // 4
        lax.fori_loop(total, padded * 4, blank, 0)
        table[6, first] = padded
    most[0] = largest


def make_table(room, place, up_count, up_row, up_col, down_count, down_row, down_col, held=()):
    def kernel(*refs):
        table_kernel(room, *refs[:7], *refs[7 + len(held):])

    outs = [jax.ShapeDtypeStruct((8, LIST), jnp.int32), jax.ShapeDtypeStruct((1,), jnp.int32)]
    return call(kernel, outs, [S] * 7 + [V] * len(held), [S] * 2, [], "table", 3)(
        place, up_count, up_row, up_col, down_count, down_row, down_col, *held
    )


def lane(index):
    return pl.ds(pl.multiple_of(index * BLK, BLK), BLK)


def in_groups(groups, run, sizes=(3, 1)):
    done = 0
    for size in sizes:
        steps = (groups - done) // size

        def step(i, unused, size=size, done=done):
            run((done + i * size) * 4, size * 4)
            return unused

        lax.fori_loop(0, steps, step, 0)
        done = done + steps * size


def block_products(table, first, take, give, left, tiles, out, contract, offset=0):
    def run(start, count):
        products = [
            lax.dot_general(
                left[:, lane(table[take, start + u])],
                tiles[table[first, start + u]],
                (((1,), (contract,)), ((), ())),
                preferred_element_type=jnp.float32,
            )
            for u in range(count)
        ]
        for u in range(count):
            out[:, lane(table[give, start + u] + offset)] += products[u]

    in_groups(table[6, first], run)


def fetch_tiles(room, sources, target, sems):
    copies = [
        pltpu.make_async_copy(source, target.at[pl.ds(far * room + first, size)], sems.at[i])
        for i, ((far, first, size), source) in enumerate(zip(pieces(room), sources))
    ]
    for copy in copies:
        copy.start()
    target[SIDE * room] = jnp.zeros((BLK, BLK), jnp.bfloat16)
    return copies


def term_parts(room):
    half = room // 2
    return (
        (0, 0, 0, room),
        (1, 0, 2 * room, half),
        (1, half, room + half, half),
        (2, 0, 2 * room + half, half),
        (2, half, 3 * room, half),
        (3, 0, room, half),
        (4, 0, 3 * room + half, half),
    )


def main_kernel(room, place, table, acts, grads, *refs):
    ups, downs = refs[:5], refs[5:10]
    partial_out, up_outs, down_outs = refs[10], refs[11:16], refs[16:21]
    up_tiles, down_tiles, sums, activated, hidden_grad, shares, sems = refs[21:]
    up_copies = fetch_tiles(room, ups, up_tiles, sems.at[0])
    down_copies = fetch_tiles(room, downs, down_tiles, sems.at[1])
    sums[...] = jnp.zeros_like(sums)
    for copy in up_copies:
        copy.wait()
    columns = activated.shape[1] // BLK
    block_products(table, 0, 1, 2, acts, up_tiles, sums, 0)
    for copy in down_copies:
        copy.wait()
    block_products(table, 3, 5, 4, grads, down_tiles, sums, 1, columns)

    def bend(i, unused):
        for row in range(0, sums.shape[0], 64):
            rows = slice(row, row + 64)
            value, slope = gelu_parts(sums[rows, lane(i)])
            activated[rows, lane(i)] = value.astype(jnp.bfloat16)
            hidden_grad[rows, lane(i)] = (sums[rows, lane(i + columns)] * slope).astype(jnp.bfloat16)
        zero = jnp.zeros((sums.shape[0], BLK), jnp.float32)
        sums[:, lane(i)] = zero
        sums[:, lane(i + columns)] = zero
        return unused

    lax.fori_loop(0, columns, bend, 0)
    block_products(table, 0, 2, 1, hidden_grad, up_tiles, sums, 1)
    def round_two(i, unused):
        at = pl.ds(pl.multiple_of(i * 2 * BLK, BLK), 2 * BLK)
        shares[:, at] = sums[:, at].astype(jnp.bfloat16)
        return unused

    lax.fori_loop(0, columns, round_two, 0)
    copies = [pltpu.make_async_copy(shares, partial_out, sems.at[2, 2])]
    copies[0].start()
    for which, (left, right, terms, outs) in enumerate(
        ((acts, hidden_grad, up_tiles, up_outs), (activated, grads, down_tiles, down_outs))
    ):
        first = which * 3

        def run(start, count, first=first, left=left, right=right, terms=terms):
            for at in range(count):
                at = start + at
                terms[table[first, at]] = lax.dot_general(
                    left[:, lane(table[first + 1, at])],
                    right[:, lane(table[first + 2, at])],
                    (((0,), (0,)), ((), ())),
                    preferred_element_type=jnp.float32,
                ).astype(jnp.bfloat16)

        in_groups(table[6, first], run, (6, 3, 1))
        for i, (out, to, start, size) in enumerate(term_parts(room)):
            copies.append(
                pltpu.make_async_copy(
                    terms.at[pl.ds(start, size)], outs[out].at[pl.ds(to, size)], sems.at[which, i]
                )
            )
            copies[-1].start()
    for copy in copies:
        copy.wait()


def unpack_kernel(room, place, up_count, down_count, *refs):
    y, x = place[0], place[1]
    half = room // 2
    for owner_of, count, ins, outs in (
        (up_owner, up_count, refs[:5], refs[10:15]),
        (down_owner, down_count, refs[5:10], refs[15:20]),
    ):
        own, from_fore, from_back, rest_fore, rest_back = ins
        position = 0
        for out, to, start, size in sorted(term_parts(CAP), key=lambda part: part[2]):
            near, start = start // CAP, start % CAP
            live = jnp.clip(count[owner_of(y, x, 0, near)] - start, 0, size)
            live = jnp.minimum(live, room - position)
            low = jnp.clip(half - position, 0, live)

            def put_low(j, at, out=outs[out], to=to, own=own, first=rest_fore, second=from_back):
                out[to + j] = add(own[at], first[at], second[half + at])
                return at + 1

            def put_high(j, at, out=outs[out], to=to, own=own, first=from_fore, second=rest_back):
                out[to + j] = add(own[at], first[at], second[at - half])
                return at + 1

            position = lax.fori_loop(0, low, put_low, position)
            position = lax.fori_loop(low, live, put_high, position)


def finish_kernel(place, up_count, down_count, up_factor, down_factor, *refs):
    owner = place[0] * SIDE + place[1]
    half = CAP // 2
    for count, factor, ins, out in (
        (up_count, up_factor, refs[:5], refs[10]),
        (down_count, down_factor, refs[5:10], refs[11]),
    ):
        own, from_fore, from_back, rest_fore, rest_back = ins
        live = count[owner]
        for j in range(CAP):
            if j < half:
                items = (own[j], rest_fore[j], from_back[half + j])
            else:
                items = (own[j], from_fore[j], rest_back[j - half])
            total = sum(item.astype(jnp.float32) for item in items) * factor[j]
            out[j] = jnp.where(j < live, total, 0.0).astype(jnp.bfloat16)


def gather_far(room, place, up_count, down_count, near_up, near_down, flag=None):
    def kernel(*refs):
        pack_kernel(room, *refs)

    packed_up, packed_down = call(
        kernel, [blocks(room)] * 2, [S] * 3 + [V] * 10, [V] * 2, [], "pack", 3
    )(place, up_count, down_count, *near_up, *near_down)
    if flag is not None:
        flag, packed_up, packed_down = lax.optimization_barrier((flag, packed_up, packed_down))
    return spread([(packed_up, over_y), (packed_down, over_x)], flag)


def layer(room, place, table, far_up, far_down, activations, output_grad, up_factor, down_factor, up_count, down_count):
    tokens, width = activations.shape
    hidden_width = FF // lax.axis_size("tensor")
    tiles = pltpu.VMEM((SIDE * room + 1, BLK, BLK), jnp.bfloat16)
    parts = [blocks(room)] * 3 + [blocks(room // 2)] * 2

    def main(*refs):
        main_kernel(room, *refs)

    def unpack(*refs):
        unpack_kernel(room, *refs)

    partial, up0, up1, up2, up3, up4, down0, down1, down2, down3, down4 = call(
        main,
        [jax.ShapeDtypeStruct((tokens, width), jnp.bfloat16)] + parts * 2,
        [S, S, V, V] + [A] * 10,
        [A] * 11,
        [tiles, tiles, pltpu.VMEM((tokens, 2 * hidden_width), jnp.float32)]
        + [pltpu.VMEM((tokens, hidden_width), jnp.bfloat16)] * 2
        + [pltpu.VMEM((tokens, width), jnp.bfloat16), pltpu.SemaphoreType.DMA((3, 8))],
        "main", 40, 38 if room == ROOM else 60,
    )(place, table, activations, output_grad, *far_up, *far_down)
    input_grad = lax.psum_scatter(partial, "tensor", scatter_dimension=1, tiled=True)
    far_up_terms, far_down_terms = collect(
        [(up0, up1, up2, up3, up4, over_y), (down0, down1, down2, down3, down4, over_x)]
    )
    caps = [blocks(CAP)] * 3 + [blocks(CAP // 2)] * 2
    sums = call(
        unpack, caps * 2, [S] * 3 + [V] * 10, [V] * 10, [], "unpack", 4
    )(place, up_count, down_count, *far_up_terms, *far_down_terms)
    near_up, near_down = collect([(*sums[:5], over_x), (*sums[5:], over_y)])
    up_grad, down_grad = call(
        finish_kernel, [blocks(CAP)] * 2, [S] * 5 + [V] * 10, [V] * 2, [], "finish", 3
    )(place, up_count, down_count, up_factor, down_factor, *near_up, *near_down)
    return input_grad, up_grad[None], down_grad[None]


def on_device(
    activations,
    output_grad,
    up_blocks,
    up_scale,
    down_blocks,
    down_scale,
    up_row_block,
    up_col_block,
    down_row_block,
    down_col_block,
    up_count,
    down_count,
):
    me, shard = lax.axis_index("fsdp"), lax.axis_index("tensor")
    place = jnp.stack([me // SIDE, me % SIDE, shard // 2, shard % 2]).astype(jnp.int32)
    up_count, down_count = up_count[0], down_count[0]
    names = (up_count, up_row_block[0], up_col_block[0], down_count, down_row_block[0], down_col_block[0])
    grad_norm = float(activations.shape[0] * lax.axis_size("fsdp")) ** (-0.5)
    wide = (activations, output_grad)
    rest = (
        up_scale[0].astype(jnp.float32) * grad_norm,
        down_scale[0].astype(jnp.float32) * grad_norm,
        up_count,
        down_count,
    )
    scaled_up = up_blocks[0] * up_scale[0][:, None, None]
    scaled_down = down_blocks[0] * down_scale[0][:, None, None]
    activations = pltpu.with_memory_space_constraint(activations, pltpu.VMEM)
    output_grad = pltpu.with_memory_space_constraint(output_grad, pltpu.VMEM)
    table, most = make_table(ROOM, place, *names, held=(activations, output_grad))
    (near_up, near_down), (table, most) = spread(
        [(scaled_up, over_x), (scaled_down, over_y)], held=(table, most)
    )
    (far_up, far_down), most = gather_far(ROOM, place, up_count, down_count, near_up, near_down, most)
    crowded = most[0] > ROOM
    results = layer(ROOM, place, table, far_up, far_down, activations, output_grad, *rest)

    def full(results, near_up, near_down, *rest):
        room = SIDE * CAP
        far_up, far_down = gather_far(room, place, up_count, down_count, near_up, near_down)
        return layer(room, place, make_table(room, place, *names)[0], far_up, far_down, *rest)

    return lax.cond(
        crowded, full, lambda results, *unused: results, results, near_up, near_down, wide[0], wide[1], *rest
    )


def solution(mesh):
    return jax.shard_map(
        on_device,
        mesh=mesh,
        in_specs=(
            P("fsdp", None),
            P("fsdp", None),
            P("tensor", "fsdp", None, None),
            P("tensor", "fsdp"),
            P("tensor", "fsdp", None, None),
            P("tensor", "fsdp"),
            P("tensor", None),
            P("tensor", None),
            P("tensor", None),
            P("tensor", None),
            P("tensor", None),
            P("tensor", None),
        ),
        out_specs=(
            P("fsdp", "tensor"),
            P("tensor", "fsdp", None, None),
            P("tensor", "fsdp", None, None),
        ),
        check_vma=False,
    )
```
